256 devices in a mesh: ctx: 32 (over z_lo, x, core), tp: 8 (over y, z_hi).
Axes of the slice: x: 4, y: 4, z: 8 (z_hi: 2, z_lo: 4; z = z_hi * 4 + z_lo), core: 2. Of those that a mesh axis runs over, the one named last changes fastest.
Arguments:
- query_heads: bfloat16 [8192, 4096], P('ctx', 'tp'), may hold values from -8 to 8
- key_heads: bfloat16 [8192, 4096], P('ctx', 'tp'), may hold values from -8 to 8
- value_heads: bfloat16 [8192, 4096], P('ctx', 'tp'), may hold values from -6 to 6
- grad_heads: bfloat16 [8192, 4096], P('ctx', 'tp'), may hold values from -6 to 6
- counts: int32 [32], replicated, may hold values from 1 to 256, as said below
Outputs:
- attended: bfloat16 [8192, 4096], P('ctx', 'tp')
- grad_query: bfloat16 [8192, 4096], P('ctx', 'tp')
- grad_key: bfloat16 [8192, 4096], P('ctx', 'tp')
- grad_value: bfloat16 [8192, 4096], P('ctx', 'tp')
The draws below stay inside these ranges and needn't reach their ends.
Inputs may be any that keep to these rules, and one draw needn't show every extreme that they name: counts[s] is the number of kept slots of shard s, which are its first ones; some shard is full in every draw.
All inputs are finite; a program needn't handle non-finite values.
Results may differ from the reference program's by a relative error of at most 0.03.
Values may be sent and summed in bfloat16 or wider, within the bound.
A program may use at most 192 MiB of HBM per device.

```python
import jax
import jax.numpy as jnp
from jax import lax

HEADS = 32
HD = 128
CAP = 256
SLOTS = 8192


def draw_query_heads(key, part):
    key = jax.random.fold_in(key, 11)
    value_key = jax.random.fold_in(key, 0)
    values = jnp.clip(jax.random.normal(value_key, (SLOTS, HEADS * HD), jnp.float32), -4.0, 4.0)
    return values.astype(jnp.bfloat16)


def draw_key_heads(key, part):
    key = jax.random.fold_in(key, 17)
    value_key = jax.random.fold_in(key, 0)
    values = jnp.clip(jax.random.normal(value_key, (SLOTS, HEADS * HD), jnp.float32), -4.0, 4.0)
    return values.astype(jnp.bfloat16)


def draw_counts(key, part):
    key = jax.random.fold_in(key, 23)
    light_key, heavy_key, pick_key, full_key = jax.random.split(key, 4)
    groups = SLOTS // CAP
    light = jax.random.randint(light_key, (groups,), 1, CAP // 2 + 1)
    heavy = CAP - jax.random.randint(heavy_key, (groups,), 0, CAP // 4 + 1)
    picked = jax.random.randint(pick_key, (groups,), 0, 2) == 0
    kept = jnp.where(picked, heavy, light)
    full_shard = jax.random.randint(full_key, (), 0, groups)
    kept = kept.at[full_shard].set(CAP)
    return kept.astype(jnp.int32)


def steps_of(stream_key, shape, cuts, smallest, high):
    def one(dim, parts):
        draws = jax.random.uniform(jax.random.fold_in(jax.random.fold_in(stream_key, 6), dim), (parts,), jnp.float32, smallest / len(cuts), high / len(cuts))
        return jnp.repeat(jnp.exp(draws), shape[dim] // parts).reshape((-1,) + (1,) * (len(shape) - dim - 1))

    level = one(*cuts[0])
    for cut in cuts[1:]:
        level = level * one(*cut)
    return level


def bell_draw(own_key, extent, scale, reach, pieces=(), kind=jnp.bfloat16):
    drawn = scale * jax.random.normal(own_key, extent, jnp.float32)
    if pieces:
        drawn = drawn * steps_of(own_key, extent, pieces, -0.22, 0.18)
    return jnp.clip(drawn, -reach, reach).astype(kind)


def setup_inputs(seed: int = 0) -> dict:
    splits = jax.random.split(jax.random.key(seed), 6)
    return {
        "query_heads": draw_query_heads(jax.random.fold_in(splits[5], 71), 0),
        "key_heads": draw_key_heads(jax.random.fold_in(splits[5], 71), 0),
        "value_heads": bell_draw(splits[2], (SLOTS, HEADS * HD), 1.0, 6.0, ((0, 32), (1, 8))),
        "grad_heads": bell_draw(splits[3], (SLOTS, HEADS * HD), 1.0, 6.0, ((0, 32), (1, 8))),
        "counts": draw_counts(jax.random.fold_in(splits[5], 71), 0),
    }


far_away = 1073741824
very_low = -1.0e30


def effective(counts, fill_value):
    slot_index = lax.iota(jnp.int32, SLOTS)
    kept_limit = jnp.repeat(counts, CAP, total_repeat_length=SLOTS)
    return jnp.where(slot_index % CAP < kept_limit, slot_index, fill_value)


def reference(query_heads, key_heads, value_heads, grad_heads, counts):
    softmax_scale = HD ** -0.5
    query_pos = effective(counts, -1)
    key_pos = effective(counts, far_away)
    allowed = key_pos[None, :] <= query_pos[:, None]
    live_rows = query_pos >= 0

    def one_head(head_index):
        column = head_index * HD
        query_part = lax.dynamic_slice_in_dim(query_heads, column, HD, 1)
        key_part = lax.dynamic_slice_in_dim(key_heads, column, HD, 1)
        value_part = lax.dynamic_slice_in_dim(value_heads, column, HD, 1)
        grad_part = lax.dynamic_slice_in_dim(grad_heads, column, HD, 1)
        scores = jnp.dot(query_part, key_part.T, preferred_element_type=jnp.float32) * softmax_scale
        row_best = jnp.max(jnp.where(allowed, scores, very_low), axis=1)
        weight_sum = jnp.sum(jnp.where(allowed, jnp.exp(scores - row_best[:, None]), 0.0), axis=1)
        log_sum = jnp.where(live_rows, row_best + jnp.log(jnp.where(live_rows, weight_sum, 1.0)), 0.0)
        soft_probs = jnp.where(allowed, jnp.exp(scores - log_sum[:, None]), 0.0)
        rounded = soft_probs.astype(jnp.bfloat16)
        attended = jnp.dot(rounded, value_part, preferred_element_type=jnp.float32).astype(jnp.bfloat16)
        row_delta = jnp.sum(attended.astype(jnp.float32) * grad_part.astype(jnp.float32), axis=1)
        grad_probs = jnp.dot(grad_part, value_part.T, preferred_element_type=jnp.float32)
        grad_scores = (soft_probs * (grad_probs - row_delta[:, None])).astype(jnp.bfloat16)
        grad_query = (jnp.dot(grad_scores, key_part, preferred_element_type=jnp.float32) * softmax_scale).astype(jnp.bfloat16)
        grad_key = (jnp.dot(grad_scores.T, query_part, preferred_element_type=jnp.float32) * softmax_scale).astype(jnp.bfloat16)
        grad_value = jnp.dot(rounded.T, grad_part, preferred_element_type=jnp.float32).astype(jnp.bfloat16)
        return attended, grad_query, grad_key, grad_value

    stacked = lax.map(one_head, lax.iota(jnp.int32, HEADS))

    def merge_heads(per_head):
        return jnp.transpose(per_head, (1, 0, 2)).reshape(SLOTS, HEADS * HD)

    return (merge_heads(stacked[0]), merge_heads(stacked[1]), merge_heads(stacked[2]), merge_heads(stacked[3]))
```

```python
import functools

import jax
import jax.numpy as jnp
from jax import lax
from jax.experimental import pallas as pl
from jax.experimental.pallas import tpu as pltpu
from jax.sharding import PartitionSpec as P

HD = 128
NZ, NX, NC = 4, 4, 2
NS = NX * NC
BR = 16
SB = 8
SEG = SB * BR
CAP = 2 * SEG
GROUP = NS * SEG
KEYS = NZ * NC * GROUP
UNIT = NC * 2 * SEG
T = 512
SIZES = (512, 640, 768, 1024)
FAR = 1e30
BIG = 1 << 30
SCALE = HD ** (-0.5)
SCALE2 = SCALE * 1.4426950408889634
MESH = pl.DeviceIdType.MESH
VMEM_BYTES = 56 * 1024 * 1024
SMEM = pl.BlockSpec(memory_space=pltpu.SMEM)
VMEM = pl.BlockSpec(memory_space=pltpu.VMEM)
HBM = pl.BlockSpec(memory_space=pltpu.HBM)
NT = (((1,), (1,)), ((), ()))
NN = (((1,), (0,)), ((), ()))


def dot(a, b, dims):
    return lax.dot_general(a, b, dims, preferred_element_type=jnp.float32)


def place():
    me = lax.axis_index("ctx")
    tp = lax.axis_index("tp")
    return me // (NC * NX), lax.rem(me // NC, NX), lax.rem(me, NC), tp


def ctx_of(z, x, core):
    return (z * NX + x) * NC + core


def cols(i):
    return pl.ds(pl.multiple_of(i * HD, HD), HD)


def remote(src, dst, ssem, rsem, dev):
    return pltpu.make_async_remote_copy(
        src_ref=src, dst_ref=dst, send_sem=ssem, recv_sem=rsem, device_id=dev, device_id_type=MESH
    )


def live_blocks(counts, p, c, j):
    nb = (counts[p * NS + j] + BR - 1) // BR
    return (nb + 1 - lax.rem(c + j, NC)) // 2


def attend_kernel(
    q, k, v, g, counts_hbm,
    kv_out, qg_out, att, st_out, info_out, col_out,
    kvs, qgs, stage, kvp, qgp, stv, info, col, oc, m_ref, l_ref, acc, qpos_ref, counts, table,
    csem, loc, sa, ra, sown, sso, rso, sfw, ssf, rz, rs, sst, rst, sat, rat, lat, okv, oqg, ost,
):
    z, x, core, tp = place()
    here = x * NC + core
    sib = (ctx_of(z, x, 1 - core), tp)
    above = (ctx_of(lax.rem(z + 1, NZ), x, core), tp)
    below = (ctx_of(lax.rem(z + NZ - 1, NZ), x, core), tp)
    has_up = z < NZ - 1
    has_dn = z > 0
    counts_copy = pltpu.make_async_copy(counts_hbm, counts, csem)
    counts_copy.start()
    partners = [(dx, dc) for dx in (0, 1, 3, 2) for dc in range(NC) if dx + dc > 0]

    def mate(dx, dc):
        return lax.rem(x + dx, NX), lax.rem(core + dc, NC)

    srcs = ((k, kvs, 0), (v, kvs, 1), (q, qgs, 0), (g, qgs, 1))
    own_parity = lax.rem(core + here, NC)
    own = []
    for a, (src, dst, part) in enumerate(srcs):
        cp = pltpu.make_async_copy(src.at[:, own_parity, :, cols(x)], dst.at[z, core, here, part], loc.at[a])
        cp.start()
        own.append(cp)

    barrier = pltpu.get_barrier_semaphore()
    for dx, dc in partners:
        px, pc = mate(dx, dc)
        pl.semaphore_signal(barrier, inc=1, device_id=(ctx_of(z, px, pc), tp), device_id_type=MESH)
    for dz in range(1, NZ):
        for pc in range(NC):
            pl.semaphore_signal(
                barrier, inc=1, device_id=(ctx_of(lax.rem(z + dz, NZ), x, pc), tp), device_id_type=MESH
            )
    pl.semaphore_wait(barrier, len(partners) + (NZ - 1) * NC)

    sends = []
    for dx, dc in partners:
        px, pc = mate(dx, dc)
        parity = lax.rem(pc + here, NC)
        for a, (src, dst, part) in enumerate(srcs):
            cp = remote(
                src.at[:, parity, :, cols(px)],
                dst.at[z, pc, here, part],
                sa.at[a, dx, dc],
                ra.at[a, dx, dc],
                (ctx_of(z, px, pc), tp),
            )
            cp.start()
            sends.append(cp)

    lane = lax.broadcasted_iota(jnp.int32, (8, SEG), 1)
    for j in range(NS):
        inside = (2 * (lane // BR) + lax.rem(core + j, NC)) * BR + lax.rem(lane, BR)
        qpos_ref[:, j * SEG : (j + 1) * SEG] = (z * NS + j) * CAP + inside
    m_ref[...] = jnp.full(m_ref.shape, -FAR, jnp.float32)
    l_ref[...] = jnp.zeros_like(l_ref)
    acc[...] = jnp.zeros_like(acc)
    counts_copy.wait()
    wide_lane = lax.broadcasted_iota(jnp.int32, (8, GROUP), 1)
    wide_sub = lax.broadcasted_iota(jnp.int32, (8, GROUP), 0)

    def begins(p, c):
        at = [jnp.int32(0)]
        for j in range(NS):
            at.append(at[-1] + live_blocks(counts, p, c, j))
        return at

    def describe(n, _):
        p, c = n // NC, lax.rem(n, NC)
        at = begins(p, c)

        def source(b, _):
            shift = jnp.int32(0)
            for j in range(1, NS):
                shift = jnp.where(b >= at[j], j * SB - at[j], shift)
            table[n * (GROUP // BR) + b] = jnp.minimum(b + shift, GROUP // BR - 1)
            return 0

        lax.fori_loop(0, GROUP // BR, source, 0)
        start = jnp.zeros_like(wide_lane)
        shift = jnp.zeros_like(wide_lane) + c * BR
        kept = jnp.zeros_like(wide_lane) + counts[p * NS]
        for j in range(1, NS):
            inside = wide_lane >= at[j] * BR
            start = jnp.where(inside, at[j] * BR, start)
            shift = jnp.where(inside, j * CAP + lax.rem(c + j, NC) * BR, shift)
            kept = jnp.where(inside, j * CAP + counts[p * NS + j], kept)
        t = wide_lane - start
        pos = t + (t // BR) * BR + shift
        bias = jnp.where(pos < kept, 0.0, -FAR)
        info[p, c] = jnp.where(wide_sub == 0, bias, (pos + p * (NS * CAP)).astype(jnp.float32))
        return 0


    def pack(buf, dst, p):
        def group(c, _):
            stage[...] = buf[p, c]

            def step(i, _):
                for b in range(8):
                    n = table[(p * NC + c) * (GROUP // BR) + i * 8 + b]
                    j, r = n // SB, lax.rem(n, SB)
                    for part in range(2):
                        dst[p, c, part, i * 8 + b] = stage[j, part, r]
                return 0

            lax.fori_loop(0, GROUP // BR // 8, step, 0)
            return 0

        lax.fori_loop(0, NC, group, 0)

    def chunk(buf, p, c, xs):
        return buf.at[p, c, pl.ds(2 * xs, 2)]

    def unit(p, xs):
        inner = lax.broadcasted_iota(jnp.int32, (SEG, 1), 0)
        ks, vs, keys = [], [], []
        for c in range(NC):
            both = kvs[p, c, pl.ds(2 * xs, 2)]
            ks.append(both[:, 0].reshape(2 * SEG, HD))
            vs.append(both[:, 1].reshape(2 * SEG, HD))
            for jj in range(2):
                inside = (2 * (inner // BR) + (c + jj) % 2) * BR + lax.rem(inner, BR)
                live = inside < counts[p * NS + 2 * xs + jj]
                keys.append(jnp.where(live, (p * NS + 2 * xs + jj) * CAP + inside, BIG))
        kk = jnp.concatenate(ks, axis=0)
        vt = jnp.concatenate(vs, axis=0).T
        key = jnp.concatenate(keys, axis=0)
        s = dot(kk, qgs[z, core, :, 0].reshape(GROUP, HD), NT) * SCALE2
        s = jnp.where(key <= qpos_ref[0:1, :], s, -FAR)
        m = m_ref[0:1, :]
        new = jnp.maximum(m, jnp.max(s, axis=0, keepdims=True))
        pr = jnp.exp2(s - new)
        f = jnp.exp2(m - new)
        m_ref[0:1, :] = new
        l_ref[0:1, :] = l_ref[0:1, :] * f + jnp.sum(pr, axis=0, keepdims=True)
        acc[...] = acc[...] * f + dot(vt, pr.astype(jnp.bfloat16), NN)

    flows = ((kvs, -1, has_up, above), (qgs, 1, has_dn, below))

    def place_of(t):
        m = lax.rem(t, NX)
        return t // NX, m, lax.rem(x + NX - (m + m // 2 - 2 * (m // 3)), NX)

    def own_comm(m):
        _, _, xs = place_of(m)
        dx = lax.rem(x + NX - xs, NX)
        for half, (buf, _, has, dev) in enumerate(flows):
            for part in range(2):
                a = 2 * half + part
                for dc in range(NC):
                    ref = buf.at[z, core, xs * NC + lax.rem(core + dc, NC), part]
                    if dc == 0:

                        @pl.when(m == 0)
                        def _():
                            own[a].wait()

                        @pl.when(m > 0)
                        def _():
                            remote(ref, ref, sa.at[a, dx, dc], ra.at[a, dx, dc], sib).wait_recv()

                    else:
                        remote(ref, ref, sa.at[a, dx, dc], ra.at[a, dx, dc], sib).wait_recv()
            ref = chunk(buf, z, core, xs)

            @pl.when(has)
            def _():
                remote(ref, ref, sown.at[half, m], rz.at[z, m], dev).start()

            remote(ref, ref, sso.at[half, m], rso.at[half, m], sib).start()

    def comm(t):
        d, m, xs = place_of(t)
        for buf, sign, has, dev in flows:
            p = z + sign * (d + 1)

            @pl.when((p >= 0) & (p < NZ))
            def _():
                ref = chunk(buf, p, core, xs)
                remote(ref, ref, sfw.at[p, m], rz.at[p, m], sib).wait_recv()

                @pl.when(has)
                def _():
                    remote(ref, ref, sfw.at[p, m], rz.at[p, m], dev).start()

                remote(ref, ref, ssf.at[p, m], rs.at[p, m], sib).start()

    def work(u, _):
        d, m, xs = place_of(u)

        @pl.when(d == 0)
        def _():
            for half, (buf, _, has, dev) in enumerate(flows):
                ref = chunk(buf, z, 1 - core, xs)
                remote(ref, ref, sso.at[half, m], rso.at[half, m], sib).wait_recv()

        for buf, sign, has, dev in flows:
            p = z + sign * d

            @pl.when((d > 0) & (p >= 0) & (p < NZ))
            def _():
                ref = chunk(buf, p, 1 - core, xs)
                remote(ref, ref, ssf.at[p, m], rs.at[p, m], sib).wait_recv()

        @pl.when(z - d >= 0)
        def _():
            unit(z - d, xs)

        whole = (m == NX - 1) & (d < NZ - 1)

        @pl.when(whole & (z - d >= 0))
        def _():
            pack(kvs, kvp, z - d)

        @pl.when(whole & (z + d < NZ))
        def _():
            pack(qgs, qgp, z + d)

        return 0

    def own_step(m, _):
        own_comm(m)
        describe(2 * m, 0)
        describe(2 * m + 1, 0)
        return 0

    def step(t, _):
        @pl.when(t < (NZ - 1) * NX)
        def _():
            comm(t)

        lax.fori_loop(jnp.where(t < 3, 2 * t, t + 3), jnp.where(t < 3, 2 * t + 2, t + 4), work, 0)
        return 0

    lax.fori_loop(0, NX, own_step, 0)
    lax.fori_loop(0, (NZ - 1) * NX + 1, step, 0)

    sub = lax.broadcasted_iota(jnp.int32, (8, SEG), 0)
    at = begins(z, core)
    packed = jnp.where(wide_sub == 0, FAR, 0.0)
    for j in range(NS):
        rows = slice(j * SEG, (j + 1) * SEG)
        live = qpos_ref[0:1, rows] - (z * NS + j) * CAP < counts[z * NS + j]
        l = l_ref[0:1, rows]
        o = jnp.where(live, acc[:, rows] / l, 0.0).T.astype(jnp.bfloat16)
        oc[j] = o.reshape(SB, BR, HD)
        cot = qgs[z, core, j, 1].reshape(SEG, HD).astype(jnp.float32)
        delta = jnp.sum(o.astype(jnp.float32) * cot, axis=1, keepdims=True)
        lse = jnp.where(live, m_ref[0:1, rows] + jnp.log2(l), FAR)
        both = jnp.where(sub == 0, lse, jnp.broadcast_to(delta, (SEG, HD)).T[:8, :])
        both = jnp.concatenate([both, jnp.zeros((8, GROUP - SEG), jnp.float32)], axis=1)
        inside = (wide_lane >= at[j] * BR) & (wide_lane < at[j + 1] * BR)
        packed = jnp.where(inside, pltpu.roll(both, at[j] * BR, 1), packed)
    stv[z, core] = packed
    for j in range(NS):
        rows = slice(j * SEG, (j + 1) * SEG)
        block = jnp.concatenate([packed[:, rows], jnp.zeros((SEG - 8, SEG), jnp.float32)], axis=0)
        col[rows, :] = block.T

    stats = stv.at[z, core]
    remote(stats, stats, sst.at[0], rst.at[z, core], sib).start()
    for dz in range(1, NZ):

        @pl.when(z - dz >= 0)
        def _():
            for pc in range(NC):
                dev = (ctx_of(z - dz, x, pc), tp)
                remote(stats, stats, sst.at[dz * NC + pc], rst.at[z, core], dev).start()

    returns = []
    for dx, dc in partners:
        px, pc = mate(dx, dc)
        there = px * NC + pc
        parity = lax.rem(core + there, NC)
        cp = remote(
            oc.at[there], att.at[x, :, parity], sat.at[dx, dc], rat.at[dx, dc], (ctx_of(z, px, pc), tp)
        )
        cp.start()
        returns.append(cp)
    stay = pltpu.make_async_copy(oc.at[here], att.at[x, :, own_parity], lat)
    stay.start()

    @pl.when(z == NZ - 1)
    def _():
        pack(kvs, kvp, 0)

    @pl.when(z == 0)
    def _():
        pack(qgs, qgp, NZ - 1)

    outs = [
        pltpu.make_async_copy(col, col_out, ost.at[NZ, 0]),
        pltpu.make_async_copy(info, info_out, ost.at[NZ, 1]),
    ]
    for buf, dst, sem in ((kvp, kv_out, okv), (qgp, qg_out, oqg)):
        outs.append(pltpu.make_async_copy(buf.at[z], dst.at[z], sem.at[z]))
    for cp in outs:
        cp.start()
    for dz in range(1, NZ):

        @pl.when(z - dz >= 0)
        def _():
            pltpu.make_async_copy(kvp.at[z - dz], kv_out.at[z - dz], okv.at[z - dz]).start()

        @pl.when(z + dz < NZ)
        def _():
            pltpu.make_async_copy(qgp.at[z + dz], qg_out.at[z + dz], oqg.at[z + dz]).start()

    pltpu.make_async_copy(stats, st_out.at[z, core], ost.at[z, core]).start()

    def take(p, c):
        ref = stv.at[p, c]
        remote(ref, ref, sst.at[0], rst.at[p, c], sib).wait_recv()
        pltpu.make_async_copy(ref, st_out.at[p, c], ost.at[p, c]).start()

    take(z, 1 - core)
    for dz in range(1, NZ):

        @pl.when(z + dz < NZ)
        def _():
            for c in range(NC):
                take(z + dz, c)

    for cp in outs:
        cp.wait()
    stay.wait()
    for dx, dc in partners:
        ox, oc_ = lax.rem(x + NX - dx, NX), lax.rem(core + NC - dc, NC)
        parity = lax.rem(oc_ + here, NC)
        ref = att.at[ox, :, parity]
        remote(oc.at[here], ref, sat.at[dx, dc], rat.at[dx, dc], sib).wait_recv()
    for cp in sends + returns:
        cp.wait_send()
    for c in range(NC):
        pltpu.make_async_copy(stv.at[z, c], st_out.at[z, c], ost.at[z, c]).wait()
    remote(stats, stats, sst.at[0], rst.at[z, core], sib).wait_send()
    for dz in range(1, NZ):

        @pl.when(z - dz >= 0)
        def _():
            pltpu.make_async_copy(kvp.at[z - dz], kv_out.at[z - dz], okv.at[z - dz]).wait()
            for pc in range(NC):
                dev = (ctx_of(z - dz, x, pc), tp)
                remote(stats, stats, sst.at[dz * NC + pc], rst.at[z, core], dev).wait_send()

        @pl.when(z + dz < NZ)
        def _():
            pltpu.make_async_copy(qgp.at[z + dz], qg_out.at[z + dz], oqg.at[z + dz]).wait()
            for c in range(NC):
                pltpu.make_async_copy(stv.at[z + dz, c], st_out.at[z + dz, c], ost.at[z + dz, c]).wait()

    for m in range(NX):
        _, _, xs = place_of(jnp.int32(m))
        for half, (buf, _, has, dev) in enumerate(flows):
            ref = chunk(buf, z, core, xs)

            @pl.when(has)
            def _():
                remote(ref, ref, sown.at[half, m], rz.at[z, m], dev).wait_send()

            remote(ref, ref, sso.at[half, m], rso.at[half, m], sib).wait_send()

    def sent(t, _):
        d, m, xs = place_of(t)
        for buf, sign, has, dev in flows:
            p = z + sign * (d + 1)

            @pl.when((p >= 0) & (p < NZ))
            def _():
                ref = chunk(buf, p, core, xs)

                @pl.when(has)
                def _():
                    remote(ref, ref, sfw.at[p, m], rz.at[p, m], dev).wait_send()

                remote(ref, ref, ssf.at[p, m], rs.at[p, m], sib).wait_send()

        return 0

    lax.fori_loop(0, (NZ - 1) * NX, sent, 0)


WHOLE = (NZ, NC, NS, 2, SB, BR, HD)
PACKED = (NZ, NC, 2, GROUP // BR, BR, HD)
ROWS = (NZ, NC, 8, GROUP)
LANDED = jax.ShapeDtypeStruct((NX, SB, 2, BR, HD), jnp.bfloat16)


def attend(q, k, v, g, counts):
    dma = pltpu.SemaphoreType.DMA
    packed = jax.ShapeDtypeStruct(PACKED, jnp.bfloat16)
    rows = jax.ShapeDtypeStruct(ROWS, jnp.float32)
    return pl.pallas_call(
        attend_kernel,
        out_shape=(
            packed,
            packed,
            LANDED,
            rows,
            rows,
            jax.ShapeDtypeStruct((GROUP, HD), jnp.float32),
        ),
        in_specs=[HBM] * 5,
        out_specs=(HBM,) * 6,
        scratch_shapes=[
            pltpu.VMEM(WHOLE, jnp.bfloat16),
            pltpu.VMEM(WHOLE, jnp.bfloat16),
            pltpu.VMEM((NS, 2, SB, BR, HD), jnp.bfloat16),
            pltpu.VMEM(PACKED, jnp.bfloat16),
            pltpu.VMEM(PACKED, jnp.bfloat16),
            pltpu.VMEM(ROWS, jnp.float32),
            pltpu.VMEM(ROWS, jnp.float32),
            pltpu.VMEM((GROUP, HD), jnp.float32),
            pltpu.VMEM((NS, SB, BR, HD), jnp.bfloat16),
            pltpu.VMEM((8, GROUP), jnp.float32),
            pltpu.VMEM((8, GROUP), jnp.float32),
            pltpu.VMEM((HD, GROUP), jnp.float32),
            pltpu.VMEM((8, GROUP), jnp.int32),
            pltpu.SMEM((NZ * NS,), jnp.int32),
            pltpu.SMEM((NZ * NC * (GROUP // BR),), jnp.int32),
            dma,
            dma((4,)),
            dma((4, NX, NC)),
            dma((4, NX, NC)),
            dma((2, NX)),
            dma((2, NX)),
            dma((2, NX)),
            dma((NZ, NX)),
            dma((NZ, NX)),
            dma((NZ, NX)),
            dma((NZ, NX)),
            dma((NZ * NC,)),
            dma((NZ, NC)),
            dma((NX, NC)),
            dma((NX, NC)),
            dma,
            dma((NZ,)),
            dma((NZ,)),
            dma((NZ + 1, NC)),
        ],
        compiler_params=pltpu.CompilerParams(
            collective_id=0, has_side_effects=True, vmem_limit_bytes=VMEM_BYTES
        ),
        name="attend",
    )(q, k, v, g, counts)


def return_kernel(count, *refs):
    ins, outs = refs[:count], refs[count : 2 * count]
    loc, ssem, rsem = refs[2 * count :]
    z, x, core, tp = place()
    here = x * NC + core
    partners = [(dx, dc) for dx in (2, 1, 3, 0) for dc in range(NC) if dx + dc > 0]
    own = []
    for a in range(count):
        cp = pltpu.make_async_copy(ins[a].at[here], outs[a].at[x, :, lax.rem(core + here, NC)], loc.at[a])
        cp.start()
        own.append(cp)
    barrier = pltpu.get_barrier_semaphore()
    for dx, dc in partners:
        dev = (ctx_of(z, lax.rem(x + dx, NX), lax.rem(core + dc, NC)), tp)
        pl.semaphore_signal(barrier, inc=1, device_id=dev, device_id_type=MESH)
    pl.semaphore_wait(barrier, len(partners))
    sends = []
    for dx, dc in partners:
        px, pc = lax.rem(x + dx, NX), lax.rem(core + dc, NC)
        there = px * NC + pc
        for a in range(count):
            cp = remote(
                ins[a].at[there],
                outs[a].at[x, :, lax.rem(core + there, NC)],
                ssem.at[a, dx, dc],
                rsem.at[a, dx, dc],
                (ctx_of(z, px, pc), tp),
            )
            cp.start()
            sends.append(cp)
    for cp in own:
        cp.wait()
    for dx, dc in partners:
        ox, oc = lax.rem(x + NX - dx, NX), lax.rem(core + NC - dc, NC)
        for a in range(count):
            ref = outs[a].at[ox, :, lax.rem(oc + here, NC)]
            remote(
                ins[a].at[here], ref, ssem.at[a, dx, dc], rsem.at[a, dx, dc], (ctx_of(z, ox, oc), tp)
            ).wait_recv()
    for cp in sends:
        cp.wait_send()


def return_heads(*arrays):
    count = len(arrays)
    dma = pltpu.SemaphoreType.DMA
    return pl.pallas_call(
        functools.partial(return_kernel, count),
        out_shape=(LANDED,) * count,
        in_specs=[HBM] * count,
        out_specs=(HBM,) * count,
        scratch_shapes=[dma((count,)), dma((count, NX, NC)), dma((count, NX, NC))],
        compiler_params=pltpu.CompilerParams(collective_id=1, has_side_effects=True),
        name="return_heads",
    )(*arrays)


def assemble_kernel(count, *refs):
    ins, outs = refs[:count], refs[count : 2 * count]
    bufs, res, lsem, ssem = refs[2 * count : 2 * count + 4]
    loads = [pltpu.make_async_copy(ins[a], bufs.at[a], lsem.at[a]) for a in range(count)]
    stores = [pltpu.make_async_copy(res.at[a], outs[a], ssem.at[a]) for a in range(count)]
    for cp in loads:
        cp.start()
    for a in range(count):
        loads[a].wait()
        for i in range(NX):
            res[a, :, i * HD : (i + 1) * HD] = bufs[a, i].reshape(CAP, HD)
        stores[a].start()
    for cp in stores:
        cp.wait()


def assemble(*arrays):
    count = len(arrays)
    dma = pltpu.SemaphoreType.DMA
    shape = jax.ShapeDtypeStruct((CAP, NX * HD), jnp.bfloat16)
    return pl.pallas_call(
        functools.partial(assemble_kernel, count),
        out_shape=(shape,) * count,
        in_specs=[HBM] * count,
        out_specs=(HBM,) * count,
        scratch_shapes=[
            pltpu.VMEM((count,) + LANDED.shape, jnp.bfloat16),
            pltpu.VMEM((count, CAP, NX * HD), jnp.bfloat16),
            dma((count,)),
            dma((count,)),
        ],
        compiler_params=pltpu.CompilerParams(vmem_limit_bytes=VMEM_BYTES),
        name="assemble",
    )(*arrays)


def fill_offsets(counts, off, z, sign, planes):
    def step(n, at):
        off[n] = at
        p, c = z + sign * (n // NC), lax.rem(n, NC)
        for j in range(NS):
            at = at + live_blocks(counts, p, c, j)
        return at

    off[planes * NC] = lax.fori_loop(0, planes * NC, step, jnp.int32(0))


def load(off, src, dst, sem, z, sign, planes, wait):
    def step(n, _):
        at = off[n]
        blocks = off[n + 1] - at
        cp = pltpu.make_async_copy(
            src.at[z + sign * (n // NC), lax.rem(n, NC), :, pl.ds(0, blocks)],
            dst.at[:, pl.ds(at, blocks)],
            sem.at[n],
        )
        if wait:
            cp.wait()
        else:
            cp.start()
        return 0

    lax.fori_loop(0, planes * NC, step, 0)


def line_up(off, src, dst, z, sign, planes, tail):
    width = GROUP + 128
    lane = lax.broadcasted_iota(jnp.int32, (8, width), 1)
    sub = lax.broadcasted_iota(jnp.int32, (8, 128), 0)

    def step(n, _):
        to = off[n] * BR
        at = pl.multiple_of((to // 128) * 128, 128)
        new = src[z + sign * (n // NC), lax.rem(n, NC)]
        new = pltpu.roll(jnp.concatenate([new, jnp.zeros((8, 128), jnp.float32)], axis=1), to - at, 1)
        old = dst[:, pl.ds(at, width)]
        dst[:, pl.ds(at, width)] = jnp.where(lane >= to - at, new, old)
        return 0

    lax.fori_loop(0, planes * NC, step, 0)
    total = off[planes * NC] * BR
    blank = jnp.where(sub == 0, tail, 0.0)
    for t in range(T // 128 + 1):
        at = pl.multiple_of((total // 128 + t) * 128, 128)
        old = dst[:, pl.ds(at, 128)]
        dst[:, pl.ds(at, 128)] = jnp.where(at + lane[:, :128] >= total, blank, old)


def backward_kernel(
    counts_hbm, qg, kv, st, info, stcol, dq_out, dk_out, dv_out,
    counts, koff, qoff, kvc, qgc, stv, infov, qrow, krow, col, dqa, dka, dva, res,
    csem, ksem, qsem, ssem, osem,
):
    z, x, core, _ = place()
    cp = pltpu.make_async_copy(counts_hbm, counts, csem)
    cp.start()
    smalls = [
        pltpu.make_async_copy(src, dst, ssem.at[i])
        for i, (src, dst) in enumerate(((st, stv), (info, infov), (stcol, col)))
    ]
    for small in smalls:
        small.start()
    cp.wait()
    kplanes, qplanes = z + 1, NZ - z
    fill_offsets(counts, koff, z, -1, kplanes)
    load(koff, kv, kvc, ksem, z, -1, kplanes, False)
    fill_offsets(counts, qoff, z, 1, qplanes)
    load(qoff, qg, qgc, qsem, z, 1, qplanes, False)
    key_end = koff[kplanes * NC]
    query_end = qoff[qplanes * NC]
    plane_end = koff[NC]
    zero = jnp.zeros((GROUP // BR, BR, HD), jnp.bfloat16)
    for part in range(2):
        kvc[part, pl.ds(key_end, GROUP // BR)] = zero
        qgc[part, pl.ds(query_end, GROUP // BR)] = zero
    for small in smalls:
        small.wait()
    line_up(koff, infov, krow, z, -1, kplanes, -FAR)
    line_up(qoff, stv, qrow, z, 1, qplanes, FAR)
    base = koff[core]
    total = koff[core + 1] - base
    starts = [jnp.int32(0)]
    for j in range(NS):
        starts.append(starts[-1] + live_blocks(counts, z, core, j))
    load(koff, kv, kvc, ksem, z, -1, kplanes, True)
    load(qoff, qg, qgc, qsem, z, 1, qplanes, True)

    def tile(buf, part, t):
        return buf[part, pl.ds(t * (T // BR), T // BR)].reshape(T, HD)

    def run(M):
        rows = pl.ds(base, M // BR)
        r = lax.broadcasted_iota(jnp.int32, (M, 1), 0)
        start = jnp.zeros_like(r)
        shift = jnp.zeros_like(r) + lax.rem(core, NC) * BR
        for j in range(1, NS):
            inside = r >= starts[j] * BR
            start = jnp.where(inside, starts[j] * BR, start)
            shift = jnp.where(inside, j * CAP + lax.rem(core + j, NC) * BR, shift)
        t = r - start
        pos = (t + (t // BR) * BR + shift + z * (NS * CAP)).astype(jnp.float32)

        dka[0:M, :] = jnp.zeros((M, HD), jnp.float32)
        dva[0:M, :] = jnp.zeros((M, HD), jnp.float32)
        dqa[0:M, :] = jnp.zeros((M, HD), jnp.float32)

        def key_step(qt, _):
            lanes = pl.ds(pl.multiple_of(qt * T, T), T)
            qb, gb = tile(qgc, 0, qt), tile(qgc, 1, qt)
            p = jnp.exp2(dot(kvc[0, rows].reshape(M, HD), qb, NT) * SCALE2 - qrow[0:1, lanes])
            n = qt * T + lax.broadcasted_iota(jnp.int32, (1, T), 1)
            there = jnp.where(n < plane_end * BR, krow[1:2, lanes], FAR)
            p = jnp.where(pos <= there, p, 0.0)
            dva[0:M, :] += dot(p.astype(jnp.bfloat16), gb, NN)
            dp = dot(kvc[1, rows].reshape(M, HD), gb, NT)
            ds = (p * (dp - qrow[1:2, lanes])).astype(jnp.bfloat16)
            dka[0:M, :] += dot(ds, qb, NN)
            return 0

        def query_step(kt, _):
            lanes = pl.ds(pl.multiple_of(kt * T, T), T)
            kb, vb = tile(kvc, 0, kt), tile(kvc, 1, kt)
            s = dot(qgc[0, rows].reshape(M, HD), kb, NT) * SCALE2 + krow[0:1, lanes]
            s = jnp.where(krow[1:2, lanes] <= pos, s, -FAR)
            p = jnp.exp2(s - col[0:M, 0:1])
            dp = dot(qgc[1, rows].reshape(M, HD), vb, NT)
            dqa[0:M, :] += dot((p * (dp - col[0:M, 1:2])).astype(jnp.bfloat16), kb, NN)
            return 0

        per = T // BR
        lax.fori_loop(0, (query_end + per - 1) // per, key_step, 0)
        lax.fori_loop(0, (key_end + per - 1) // per, query_step, 0)

    lower = 0
    for size in SIZES:

        @pl.when((total * BR > lower) & (total * BR <= size))
        def _():
            run(size)

        lower = size

    r = lax.broadcasted_iota(jnp.int32, (SEG, HD), 0)
    stores = []
    for a, (src, dst, scale) in enumerate(((dka, dk_out, SCALE), (dva, dv_out, 1.0), (dqa, dq_out, SCALE))):
        for j in range(NS):
            row = r + (r // BR + lax.rem(core + j, NC)) * BR
            part = src[pl.ds(pl.multiple_of(starts[j] * BR, BR), SEG), :] * scale
            part = jnp.where(row < counts[z * NS + j], part, 0.0)
            res[a, j] = part.astype(jnp.bfloat16).reshape(SB, BR, HD)
        cp = pltpu.make_async_copy(res.at[a], dst, osem.at[a])
        cp.start()
        stores.append(cp)
    for cp in stores:
        cp.wait()


def backward(counts, qg, kv, st, info, stcol):
    dma = pltpu.SemaphoreType.DMA
    parts = jax.ShapeDtypeStruct((NS, SB, BR, HD), jnp.bfloat16)
    blocks = (KEYS + GROUP + T) // BR
    return pl.pallas_call(
        backward_kernel,
        out_shape=(parts, parts, parts),
        in_specs=[HBM] * 6,
        out_specs=(HBM,) * 3,
        scratch_shapes=[
            pltpu.SMEM((NZ * NS,), jnp.int32),
            pltpu.SMEM((NZ * NC + 1,), jnp.int32),
            pltpu.SMEM((NZ * NC + 1,), jnp.int32),
            pltpu.VMEM((2, blocks, BR, HD), jnp.bfloat16),
            pltpu.VMEM((2, blocks, BR, HD), jnp.bfloat16),
            pltpu.VMEM(ROWS, jnp.float32),
            pltpu.VMEM(ROWS, jnp.float32),
            pltpu.VMEM((8, KEYS + GROUP + T), jnp.float32),
            pltpu.VMEM((8, KEYS + GROUP + T), jnp.float32),
            pltpu.VMEM((GROUP, HD), jnp.float32),
            pltpu.VMEM((GROUP + SEG, HD), jnp.float32),
            pltpu.VMEM((GROUP + SEG, HD), jnp.float32),
            pltpu.VMEM((GROUP + SEG, HD), jnp.float32),
            pltpu.VMEM((3, NS, SB, BR, HD), jnp.bfloat16),
            dma,
            dma((NZ * NC,)),
            dma((NZ * NC,)),
            dma((3,)),
            dma((3,)),
        ],
        compiler_params=pltpu.CompilerParams(vmem_limit_bytes=VMEM_BYTES),
        name="backward",
    )(counts, qg, kv, st, info, stcol)


def on_device(query_heads, key_heads, value_heads, grad_heads, counts):
    def blocks(array):
        return array.reshape(SB, 2, BR, NX * HD)

    kv, qg, att, st, info, stcol = attend(
        blocks(query_heads), blocks(key_heads), blocks(value_heads), blocks(grad_heads), counts
    )
    dq, dk, dv = backward(counts, qg, kv, st, info, stcol)
    return assemble(att, *return_heads(dq, dk, dv))


def solution(mesh):
    return jax.shard_map(
        on_device,
        mesh=mesh,
        in_specs=(P("ctx", "tp"), P("ctx", "tp"), P("ctx", "tp"), P("ctx", "tp"), P()),
        out_specs=(P("ctx", "tp"), P("ctx", "tp"), P("ctx", "tp"), P("ctx", "tp")),
        check_vma=False,
    )
```

```python
import functools

import jax
import jax.numpy as jnp
from jax import lax
from jax.experimental import pallas as pl
from jax.experimental.pallas import tpu as pltpu
from jax.sharding import PartitionSpec as P

HD = 128
NZ, NX, NC = 4, 4, 2
NS = NX * NC
BR = 16
SB = 8
SEG = SB * BR
CAP = 2 * SEG
GROUP = NS * SEG
KEYS = NZ * NC * GROUP
UNIT = NC * 2 * SEG
T = 512
SIZES = (640, 768, 1024)
FAR = 1e30
BIG = 1 << 30
SCALE = HD ** (-0.5)
SCALE2 = SCALE * 1.4426950408889634
MESH = pl.DeviceIdType.MESH
VMEM_BYTES = 56 * 1024 * 1024
SMEM = pl.BlockSpec(memory_space=pltpu.SMEM)
VMEM = pl.BlockSpec(memory_space=pltpu.VMEM)
HBM = pl.BlockSpec(memory_space=pltpu.HBM)
NT = (((1,), (1,)), ((), ()))
NN = (((1,), (0,)), ((), ()))


def dot(a, b, dims):
    return lax.dot_general(a, b, dims, preferred_element_type=jnp.float32)


def place():
    me = lax.axis_index("ctx")
    tp = lax.axis_index("tp")
    return me // (NC * NX), lax.rem(me // NC, NX), lax.rem(me, NC), tp


def ctx_of(z, x, core):
    return (z * NX + x) * NC + core


def cols(i):
    return pl.ds(pl.multiple_of(i * HD, HD), HD)


def remote(src, dst, ssem, rsem, dev):
    return pltpu.make_async_remote_copy(
        src_ref=src, dst_ref=dst, send_sem=ssem, recv_sem=rsem, device_id=dev, device_id_type=MESH
    )


def live_blocks(counts, p, c, j):
    nb = (counts[p * NS + j] + BR - 1) // BR
    return (nb + 1 - lax.rem(c + j, NC)) // 2


def attend_kernel(
    q, k, v, g, counts_hbm,
    kv_out, qg_out, att, st_out, info_out, col_out, dq_out, dkv_out,
    kvs, qgs, stage, dqs, dkv, kvp, qgp, stv, info, col, oc, m_ref, l_ref, acc, qpos_ref, counts, table,
    csem, loc, sa, ra, sown, sso, rso, sfw, ssf, rz, rs, sst, rst, sat, rat, lat, okv, oqg, ost, sdq, sdkv,
):
    z, x, core, tp = place()
    here = x * NC + core
    sib = (ctx_of(z, x, 1 - core), tp)
    above = (ctx_of(lax.rem(z + 1, NZ), x, core), tp)
    below = (ctx_of(lax.rem(z + NZ - 1, NZ), x, core), tp)
    has_up = z < NZ - 1
    has_dn = z > 0
    counts_copy = pltpu.make_async_copy(counts_hbm, counts, csem)
    counts_copy.start()
    partners = [(dx, dc) for dx in (0, 1, 3, 2) for dc in range(NC) if dx + dc > 0]

    def mate(dx, dc):
        return lax.rem(x + dx, NX), lax.rem(core + dc, NC)

    srcs = ((k, kvs, 0), (v, kvs, 1), (q, qgs, 0), (g, qgs, 1))
    own_parity = lax.rem(core + here, NC)
    own = []
    for a, (src, dst, part) in enumerate(srcs):
        cp = pltpu.make_async_copy(src.at[:, own_parity, :, cols(x)], dst.at[z, core, here, part], loc.at[a])
        cp.start()
        own.append(cp)

    barrier = pltpu.get_barrier_semaphore()
    for dx, dc in partners:
        px, pc = mate(dx, dc)
        pl.semaphore_signal(barrier, inc=1, device_id=(ctx_of(z, px, pc), tp), device_id_type=MESH)
    for dz in range(1, NZ):
        for pc in range(NC):
            pl.semaphore_signal(
                barrier, inc=1, device_id=(ctx_of(lax.rem(z + dz, NZ), x, pc), tp), device_id_type=MESH
            )
    pl.semaphore_wait(barrier, len(partners) + (NZ - 1) * NC)

    sends = []
    for dx, dc in partners:
        px, pc = mate(dx, dc)
        parity = lax.rem(pc + here, NC)
        for a, (src, dst, part) in enumerate(srcs):
            cp = remote(
                src.at[:, parity, :, cols(px)],
                dst.at[z, pc, here, part],
                sa.at[a, dx, dc],
                ra.at[a, dx, dc],
                (ctx_of(z, px, pc), tp),
            )
            cp.start()
            sends.append(cp)

    lane = lax.broadcasted_iota(jnp.int32, (8, SEG), 1)
    for j in range(NS):
        inside = (2 * (lane // BR) + lax.rem(core + j, NC)) * BR + lax.rem(lane, BR)
        qpos_ref[:, j * SEG : (j + 1) * SEG] = (z * NS + j) * CAP + inside
    m_ref[...] = jnp.full(m_ref.shape, -FAR, jnp.float32)
    l_ref[...] = jnp.zeros_like(l_ref)
    acc[...] = jnp.zeros_like(acc)
    dkv[...] = jnp.zeros_like(dkv)
    counts_copy.wait()
    wide_lane = lax.broadcasted_iota(jnp.int32, (8, GROUP), 1)
    wide_sub = lax.broadcasted_iota(jnp.int32, (8, GROUP), 0)

    def begins(p, c):
        at = [jnp.int32(0)]
        for j in range(NS):
            at.append(at[-1] + live_blocks(counts, p, c, j))
        return at

    def describe(n, _):
        p, c = n // NC, lax.rem(n, NC)
        at = begins(p, c)

        def source(b, _):
            shift = jnp.int32(0)
            for j in range(1, NS):
                shift = jnp.where(b >= at[j], j * SB - at[j], shift)
            table[n * (GROUP // BR) + b] = jnp.minimum(b + shift, GROUP // BR - 1)
            return 0

        lax.fori_loop(0, GROUP // BR, source, 0)
        start = jnp.zeros_like(wide_lane)
        shift = jnp.zeros_like(wide_lane) + c * BR
        kept = jnp.zeros_like(wide_lane) + counts[p * NS]
        for j in range(1, NS):
            inside = wide_lane >= at[j] * BR
            start = jnp.where(inside, at[j] * BR, start)
            shift = jnp.where(inside, j * CAP + lax.rem(c + j, NC) * BR, shift)
            kept = jnp.where(inside, j * CAP + counts[p * NS + j], kept)
        t = wide_lane - start
        pos = t + (t // BR) * BR + shift
        bias = jnp.where(pos < kept, 0.0, -FAR)
        info[p, c] = jnp.where(wide_sub == 0, bias, (pos + p * (NS * CAP)).astype(jnp.float32))
        return 0


    def pack(buf, dst, p):
        def group(c, _):
            stage[...] = buf[p, c]

            def step(i, _):
                for b in range(8):
                    n = table[(p * NC + c) * (GROUP // BR) + i * 8 + b]
                    j, r = n // SB, lax.rem(n, SB)
                    for part in range(2):
                        dst[p, c, part, i * 8 + b] = stage[j, part, r]
                return 0

            lax.fori_loop(0, GROUP // BR // 8, step, 0)
            return 0

        lax.fori_loop(0, NC, group, 0)

    def chunk(buf, p, c, xs):
        return buf.at[p, c, pl.ds(2 * xs, 2)]

    def keys_of(p, xs):
        inner = lax.broadcasted_iota(jnp.int32, (SEG, 1), 0)
        ks, vs, keys = [], [], []
        for c in range(NC):
            both = kvs[p, c, pl.ds(2 * xs, 2)]
            ks.append(both[:, 0].reshape(2 * SEG, HD))
            vs.append(both[:, 1].reshape(2 * SEG, HD))
            for jj in range(2):
                inside = (2 * (inner // BR) + (c + jj) % 2) * BR + lax.rem(inner, BR)
                live = inside < counts[p * NS + 2 * xs + jj]
                keys.append(jnp.where(live, (p * NS + 2 * xs + jj) * CAP + inside, BIG))
        kk = jnp.concatenate(ks, axis=0)
        vv = jnp.concatenate(vs, axis=0)
        s = dot(kk, qgs[z, core, :, 0].reshape(GROUP, HD), NT) * SCALE2
        return kk, vv, jnp.where(jnp.concatenate(keys, axis=0) <= qpos_ref[0:1, :], s, -FAR)

    def unit(p, xs):
        _, vv, s = keys_of(p, xs)
        m = m_ref[0:1, :]
        new = jnp.maximum(m, jnp.max(s, axis=0, keepdims=True))
        pr = jnp.exp2(s - new)
        f = jnp.exp2(m - new)
        m_ref[0:1, :] = new
        l_ref[0:1, :] = l_ref[0:1, :] * f + jnp.sum(pr, axis=0, keepdims=True)
        acc[...] = acc[...] * f + dot(vv.T, pr.astype(jnp.bfloat16), NN)

    def unit_back(p, xs):
        kk, vv, s = keys_of(p, xs)
        pr = jnp.exp2(s - m_ref[0:1, :])
        dp = dot(vv, qgs[z, core, :, 1].reshape(GROUP, HD), NT)
        ds = (pr * (dp - l_ref[0:1, :])).astype(jnp.bfloat16)
        acc[...] += dot(kk.T, ds, NN)

    def unit_key(p, xs):
        line = lax.broadcasted_iota(jnp.int32, (1, SEG), 1)
        inner = lax.broadcasted_iota(jnp.int32, (SEG, 1), 0)
        qs, gs, lses, deltas, queries, keys = [], [], [], [], [], []
        for c in range(NC):
            both = qgs[p, c, pl.ds(2 * xs, 2)]
            qs.append(both[:, 0].reshape(2 * SEG, HD))
            gs.append(both[:, 1].reshape(2 * SEG, HD))
            lanes = pl.ds(pl.multiple_of(2 * xs * SEG, 2 * SEG), 2 * SEG)
            lses.append(stv[p, c, 2:3, lanes])
            deltas.append(stv[p, c, 3:4, lanes])
            for jj in range(2):
                inside = (2 * (line // BR) + (c + jj) % 2) * BR + lax.rem(line, BR)
                queries.append((p * NS + 2 * xs + jj) * CAP + inside)
        for j in range(NS):
            keys.append(j * CAP + (2 * (inner // BR) + lax.rem(core + j, NC)) * BR + lax.rem(inner, BR))
        qq, gg = jnp.concatenate(qs, axis=0), jnp.concatenate(gs, axis=0)
        lse, delta = jnp.concatenate(lses, axis=1), jnp.concatenate(deltas, axis=1)
        s = dot(kvs[0, core, :, 0].reshape(GROUP, HD), qq, NT) * SCALE2
        pr = jnp.exp2(s - lse)
        pr = jnp.where(jnp.concatenate(keys, axis=0) <= jnp.concatenate(queries, axis=1), pr, 0.0)
        dkv[1] += dot(pr.astype(jnp.bfloat16), gg, NN)
        dp = dot(kvs[0, core, :, 1].reshape(GROUP, HD), gg, NT)
        dkv[0] += dot((pr * (dp - delta)).astype(jnp.bfloat16), qq, NN)

    flows = ((kvs, -1, has_up, above), (qgs, 1, has_dn, below))

    def place_of(t):
        m = lax.rem(t, NX)
        return t // NX, m, lax.rem(x + NX - (m + m // 2 - 2 * (m // 3)), NX)

    def own_comm(m):
        _, _, xs = place_of(m)
        dx = lax.rem(x + NX - xs, NX)
        for half, (buf, _, has, dev) in enumerate(flows):
            for part in range(2):
                a = 2 * half + part
                for dc in range(NC):
                    ref = buf.at[z, core, xs * NC + lax.rem(core + dc, NC), part]
                    if dc == 0:

                        @pl.when(m == 0)
                        def _():
                            own[a].wait()

                        @pl.when(m > 0)
                        def _():
                            remote(ref, ref, sa.at[a, dx, dc], ra.at[a, dx, dc], sib).wait_recv()

                    else:
                        remote(ref, ref, sa.at[a, dx, dc], ra.at[a, dx, dc], sib).wait_recv()
            ref = chunk(buf, z, core, xs)

            @pl.when(has)
            def _():
                remote(ref, ref, sown.at[half, m], rz.at[z, m], dev).start()

            remote(ref, ref, sso.at[half, m], rso.at[half, m], sib).start()

    def comm(t):
        d, m, xs = place_of(t)
        for buf, sign, has, dev in flows:
            p = z + sign * (d + 1)

            @pl.when((p >= 0) & (p < NZ))
            def _():
                ref = chunk(buf, p, core, xs)
                remote(ref, ref, sfw.at[p, m], rz.at[p, m], sib).wait_recv()

                @pl.when(has)
                def _():
                    remote(ref, ref, sfw.at[p, m], rz.at[p, m], dev).start()

                remote(ref, ref, ssf.at[p, m], rs.at[p, m], sib).start()

    def work(u, _):
        d, m, xs = place_of(u)

        @pl.when(d == 0)
        def _():
            for half, (buf, _, has, dev) in enumerate(flows):
                ref = chunk(buf, z, 1 - core, xs)
                remote(ref, ref, sso.at[half, m], rso.at[half, m], sib).wait_recv()

        for buf, sign, has, dev in flows:
            p = z + sign * d

            @pl.when((d > 0) & (p >= 0) & (p < NZ))
            def _():
                ref = chunk(buf, p, 1 - core, xs)
                remote(ref, ref, ssf.at[p, m], rs.at[p, m], sib).wait_recv()

        @pl.when(z - d >= 0)
        def _():
            unit(z - d, xs)

        whole = (m == NX - 1) & (d < NZ - 1)

        @pl.when(whole & ((d == 0) | (z == NZ - 1)))
        def _():
            pack(kvs, kvp, z - d)

        @pl.when(whole & (z > 0) & (z + d < NZ))
        def _():
            pack(qgs, qgp, z + d)

        return 0

    def own_step(m, _):
        own_comm(m)
        describe(2 * m, 0)
        describe(2 * m + 1, 0)
        return 0

    stats = stv.at[z, core]

    def send_stats(act):
        act(remote(stats, stats, sst.at[0], rst.at[z, core], sib))
        for dz in range(1, NZ):

            @pl.when(z - dz >= 0)
            def _():
                for pc in range(NC):
                    dev = (ctx_of(z - dz, x, pc), tp)
                    act(remote(stats, stats, sst.at[dz * NC + pc], rst.at[z, core], dev))

    def send_rows(act):
        for dx, dc in partners:
            px, pc = mate(dx, dc)
            there = px * NC + pc
            parity = lax.rem(core + there, NC)
            act(
                remote(
                    oc.at[there], att.at[x, :, parity], sat.at[dx, dc], rat.at[dx, dc], (ctx_of(z, px, pc), tp)
                )
            )

    stay = pltpu.make_async_copy(oc.at[here], att.at[x, :, own_parity], lat)

    def finish():
        sub = lax.broadcasted_iota(jnp.int32, (8, SEG), 0)
        at = begins(z, core)
        packed = jnp.where(wide_sub == 0, FAR, 0.0)
        for j in range(NS):
            rows = slice(j * SEG, (j + 1) * SEG)
            live = qpos_ref[0:1, rows] - (z * NS + j) * CAP < counts[z * NS + j]
            l = l_ref[0:1, rows]
            o = jnp.where(live, acc[:, rows] / l, 0.0).T.astype(jnp.bfloat16)
            oc[j] = o.reshape(SB, BR, HD)
            cot = qgs[z, core, j, 1].reshape(SEG, HD).astype(jnp.float32)
            delta = jnp.sum(o.astype(jnp.float32) * cot, axis=1, keepdims=True)
            lse = jnp.where(live, m_ref[0:1, rows] + jnp.log2(l), FAR)
            both = jnp.where(sub == 0, lse, jnp.broadcast_to(delta, (SEG, HD)).T[:8, :])
            m_ref[0:1, rows] = lse
            l_ref[0:1, rows] = both[1:2, :]
            both = jnp.concatenate([both, jnp.zeros((8, GROUP - SEG), jnp.float32)], axis=1)
            inside = (wide_lane >= at[j] * BR) & (wide_lane < at[j + 1] * BR)
            packed = jnp.where(inside, pltpu.roll(both, at[j] * BR, 1), packed)
        dense = jnp.where(wide_sub == 2, m_ref[0:1, :], l_ref[0:1, :])
        stv[z, core] = jnp.where(wide_sub < 2, packed, dense)
        for j in range(NS):
            rows = slice(j * SEG, (j + 1) * SEG)
            block = jnp.concatenate([packed[:, rows], jnp.zeros((SEG - 8, SEG), jnp.float32)], axis=0)
            col[rows, :] = block.T

        acc[...] = jnp.zeros_like(acc)
        send_stats(lambda cp: cp.start())
        send_rows(lambda cp: cp.start())
        stay.start()

    top = z == NZ - 1
    done = jnp.where(z == 0, 1, 4 * z)
    pace = jnp.where(z == NZ - 2, 3, 1)

    def back(u, _):
        d, m, xs = place_of(u)
        unit_back(z - d, xs)
        return 0

    def key_work(w, _):
        p, m, xs = place_of(w)
        for c in range(NC):

            @pl.when((m == 0) & ((p > 0) | (c != core)))
            def _():
                ref = stv.at[p, c]
                remote(ref, ref, sst.at[0], rst.at[p, c], sib).wait_recv()

        unit_key(p, xs)
        return 0

    def step(t, _):
        @pl.when(t < (NZ - 1) * NX)
        def _():
            comm(t)

        lax.fori_loop(jnp.where(t < 3, 2 * t, t + 3), jnp.where(t < 3, 2 * t + 2, t + 4), work, 0)

        @pl.when(t == done)
        def _():
            finish()

        @pl.when((t > done) & (z < NZ - 1))
        def _():
            first = (t - done - 1) * pace
            last = jnp.minimum(first + pace, NX * (z + 1))
            lax.fori_loop(first, last, back, 0)

        @pl.when((z == 0) & (t >= 6) & (t < 12))
        def _():
            lax.fori_loop(2 * t - 12, 2 * t - 10, key_work, 0)

        return 0

    lax.fori_loop(0, NX, own_step, 0)
    lax.fori_loop(0, (NZ - 1) * NX + 1, step, 0)

    @pl.when(z < NZ - 1)
    def _():
        for j in range(NS):
            rows = slice(j * SEG, (j + 1) * SEG)
            dqs[j] = (acc[:, rows] * SCALE).T.astype(jnp.bfloat16).reshape(SB, BR, HD)
        pltpu.make_async_copy(dqs, dq_out, sdq).start()

    @pl.when(z == 0)
    def _():
        pltpu.make_async_copy(dkv, dkv_out, sdkv).start()

    @pl.when(z == NZ - 1)
    def _():
        pack(kvs, kvp, 0)

    @pl.when(z == 0)
    def _():
        pack(qgs, qgp, NZ - 1)

    outs = [
        pltpu.make_async_copy(col, col_out, ost.at[NZ, 0]),
        pltpu.make_async_copy(info, info_out, ost.at[NZ, 1]),
    ]
    for buf, dst, sem in ((kvp, kv_out, okv), (qgp, qg_out, oqg)):
        outs.append(pltpu.make_async_copy(buf.at[z], dst.at[z], sem.at[z]))
    for cp in outs:
        cp.start()
    def copies(act, take):
        for dz in range(1, NZ):

            @pl.when((z - dz >= 0) & (z == NZ - 1))
            def _():
                act(pltpu.make_async_copy(kvp.at[z - dz], kv_out.at[z - dz], okv.at[z - dz]))

            @pl.when((z + dz < NZ) & ((z > 0) | (dz == NZ - 1)))
            def _():
                act(pltpu.make_async_copy(qgp.at[z + dz], qg_out.at[z + dz], oqg.at[z + dz]))

        @pl.when(z > 0)
        def _():
            act(pltpu.make_async_copy(stats, st_out.at[z, core], ost.at[z, core]))
            take(z, 1 - core)

        for dz in range(1, NZ):

            @pl.when((z + dz < NZ) & ((z > 0) | (dz == NZ - 1)))
            def _():
                for c in range(NC):
                    take(z + dz, c)

    def take(p, c):
        ref = stv.at[p, c]
        remote(ref, ref, sst.at[0], rst.at[p, c], sib).wait_recv()
        pltpu.make_async_copy(ref, st_out.at[p, c], ost.at[p, c]).start()

    copies(lambda cp: cp.start(), take)

    for cp in outs:
        cp.wait()
    stay.wait()
    for dx, dc in partners:
        ox, oc_ = lax.rem(x + NX - dx, NX), lax.rem(core + NC - dc, NC)
        parity = lax.rem(oc_ + here, NC)
        ref = att.at[ox, :, parity]
        remote(oc.at[here], ref, sat.at[dx, dc], rat.at[dx, dc], sib).wait_recv()
    for cp in sends:
        cp.wait_send()
    send_rows(lambda cp: cp.wait_send())
    send_stats(lambda cp: cp.wait_send())

    @pl.when(z < NZ - 1)
    def _():
        pltpu.make_async_copy(dqs, dq_out, sdq).wait()

    @pl.when(z == 0)
    def _():
        pltpu.make_async_copy(dkv, dkv_out, sdkv).wait()

    copies(
        lambda cp: cp.wait(),
        lambda p, c: pltpu.make_async_copy(stv.at[p, c], st_out.at[p, c], ost.at[p, c]).wait(),
    )

    for m in range(NX):
        _, _, xs = place_of(jnp.int32(m))
        for half, (buf, _, has, dev) in enumerate(flows):
            ref = chunk(buf, z, core, xs)

            @pl.when(has)
            def _():
                remote(ref, ref, sown.at[half, m], rz.at[z, m], dev).wait_send()

            remote(ref, ref, sso.at[half, m], rso.at[half, m], sib).wait_send()

    def sent(t, _):
        d, m, xs = place_of(t)
        for buf, sign, has, dev in flows:
            p = z + sign * (d + 1)

            @pl.when((p >= 0) & (p < NZ))
            def _():
                ref = chunk(buf, p, core, xs)

                @pl.when(has)
                def _():
                    remote(ref, ref, sfw.at[p, m], rz.at[p, m], dev).wait_send()

                remote(ref, ref, ssf.at[p, m], rs.at[p, m], sib).wait_send()

        return 0

    lax.fori_loop(0, (NZ - 1) * NX, sent, 0)


WHOLE = (NZ, NC, NS, 2, SB, BR, HD)
PACKED = (NZ, NC, 2, GROUP // BR, BR, HD)
ROWS = (NZ, NC, 8, GROUP)
LANDED = jax.ShapeDtypeStruct((NX, SB, 2, BR, HD), jnp.bfloat16)
PARTS = jax.ShapeDtypeStruct((NS, SB, BR, HD), jnp.bfloat16)
GRADS = jax.ShapeDtypeStruct((NS, 3, SB, BR, HD), jnp.bfloat16)
LANDED3 = jax.ShapeDtypeStruct((NX, 3, SB, 2, BR, HD), jnp.bfloat16)


def attend(q, k, v, g, counts):
    dma = pltpu.SemaphoreType.DMA
    packed = jax.ShapeDtypeStruct(PACKED, jnp.bfloat16)
    rows = jax.ShapeDtypeStruct(ROWS, jnp.float32)
    return pl.pallas_call(
        attend_kernel,
        out_shape=(
            packed,
            packed,
            LANDED,
            rows,
            rows,
            jax.ShapeDtypeStruct((GROUP, HD), jnp.float32),
            PARTS,
            jax.ShapeDtypeStruct((2, GROUP, HD), jnp.float32),
        ),
        in_specs=[HBM] * 5,
        out_specs=(HBM,) * 8,
        scratch_shapes=[
            pltpu.VMEM(WHOLE, jnp.bfloat16),
            pltpu.VMEM(WHOLE, jnp.bfloat16),
            pltpu.VMEM((NS, 2, SB, BR, HD), jnp.bfloat16),
            pltpu.VMEM((NS, SB, BR, HD), jnp.bfloat16),
            pltpu.VMEM((2, GROUP, HD), jnp.float32),
            pltpu.VMEM(PACKED, jnp.bfloat16),
            pltpu.VMEM(PACKED, jnp.bfloat16),
            pltpu.VMEM(ROWS, jnp.float32),
            pltpu.VMEM(ROWS, jnp.float32),
            pltpu.VMEM((GROUP, HD), jnp.float32),
            pltpu.VMEM((NS, SB, BR, HD), jnp.bfloat16),
            pltpu.VMEM((8, GROUP), jnp.float32),
            pltpu.VMEM((8, GROUP), jnp.float32),
            pltpu.VMEM((HD, GROUP), jnp.float32),
            pltpu.VMEM((8, GROUP), jnp.int32),
            pltpu.SMEM((NZ * NS,), jnp.int32),
            pltpu.SMEM((NZ * NC * (GROUP // BR),), jnp.int32),
            dma,
            dma((4,)),
            dma((4, NX, NC)),
            dma((4, NX, NC)),
            dma((2, NX)),
            dma((2, NX)),
            dma((2, NX)),
            dma((NZ, NX)),
            dma((NZ, NX)),
            dma((NZ, NX)),
            dma((NZ, NX)),
            dma((NZ * NC,)),
            dma((NZ, NC)),
            dma((NX, NC)),
            dma((NX, NC)),
            dma,
            dma((NZ,)),
            dma((NZ,)),
            dma((NZ + 1, NC)),
            dma,
            dma,
        ],
        compiler_params=pltpu.CompilerParams(
            collective_id=0, has_side_effects=True, vmem_limit_bytes=VMEM_BYTES
        ),
        name="attend",
    )(q, k, v, g, counts)


def return_kernel(grads, out, loc, ssem, rsem):
    z, x, core, tp = place()
    here = x * NC + core
    partners = [(dx, dc) for dx in (2, 1, 3, 0) for dc in range(NC) if dx + dc > 0]
    own = pltpu.make_async_copy(grads.at[here], out.at[x, :, :, lax.rem(core + here, NC)], loc)
    own.start()
    barrier = pltpu.get_barrier_semaphore()
    for dx, dc in partners:
        dev = (ctx_of(z, lax.rem(x + dx, NX), lax.rem(core + dc, NC)), tp)
        pl.semaphore_signal(barrier, inc=1, device_id=dev, device_id_type=MESH)
    pl.semaphore_wait(barrier, len(partners))
    sends = []
    for dx, dc in partners:
        px, pc = lax.rem(x + dx, NX), lax.rem(core + dc, NC)
        there = px * NC + pc
        cp = remote(
            grads.at[there],
            out.at[x, :, :, lax.rem(core + there, NC)],
            ssem.at[dx, dc],
            rsem.at[dx, dc],
            (ctx_of(z, px, pc), tp),
        )
        cp.start()
        sends.append(cp)
    own.wait()
    for dx, dc in partners:
        ox, oc = lax.rem(x + NX - dx, NX), lax.rem(core + NC - dc, NC)
        ref = out.at[ox, :, :, lax.rem(oc + here, NC)]
        remote(grads.at[here], ref, ssem.at[dx, dc], rsem.at[dx, dc], (ctx_of(z, ox, oc), tp)).wait_recv()
    for cp in sends:
        cp.wait_send()


def return_heads(grads):
    dma = pltpu.SemaphoreType.DMA
    return pl.pallas_call(
        return_kernel,
        out_shape=LANDED3,
        in_specs=[HBM],
        out_specs=HBM,
        scratch_shapes=[dma, dma((NX, NC)), dma((NX, NC))],
        compiler_params=pltpu.CompilerParams(collective_id=1, has_side_effects=True),
        name="return_heads",
    )(grads)


def assemble_kernel(att, grads, *refs):
    outs = refs[:4]
    buf0, buf, res, lsem, ssem = refs[4:]
    loads = [pltpu.make_async_copy(att, buf0, lsem.at[0])]
    loads += [pltpu.make_async_copy(grads.at[:, a], buf.at[:, a], lsem.at[a + 1]) for a in range(3)]
    for cp in loads:
        cp.start()
    stores = [pltpu.make_async_copy(res.at[a], outs[a], ssem.at[a]) for a in range(4)]
    for a in range(4):
        loads[a].wait()
        for i in range(NX):
            part = buf0[i] if a == 0 else buf[i, a - 1]
            res[a, :, i * HD : (i + 1) * HD] = part.reshape(CAP, HD)
        stores[a].start()
    for cp in stores:
        cp.wait()


def assemble(att, grads):
    dma = pltpu.SemaphoreType.DMA
    shape = jax.ShapeDtypeStruct((CAP, NX * HD), jnp.bfloat16)
    return pl.pallas_call(
        assemble_kernel,
        out_shape=(shape,) * 4,
        in_specs=[HBM] * 2,
        out_specs=(HBM,) * 4,
        scratch_shapes=[
            pltpu.VMEM(LANDED.shape, jnp.bfloat16),
            pltpu.VMEM(LANDED3.shape, jnp.bfloat16),
            pltpu.VMEM((4, CAP, NX * HD), jnp.bfloat16),
            dma((4,)),
            dma((4,)),
        ],
        compiler_params=pltpu.CompilerParams(vmem_limit_bytes=VMEM_BYTES),
        name="assemble",
    )(att, grads)


def fill_offsets(counts, off, z, sign, planes):
    def step(n, at):
        off[n] = at
        p, c = z + sign * (n // NC), lax.rem(n, NC)
        for j in range(NS):
            at = at + live_blocks(counts, p, c, j)
        return at

    off[planes * NC] = lax.fori_loop(0, planes * NC, step, jnp.int32(0))


def load(off, src, dst, sem, z, sign, planes, wait):
    def step(n, _):
        at = off[n]
        blocks = off[n + 1] - at
        cp = pltpu.make_async_copy(
            src.at[z + sign * (n // NC), lax.rem(n, NC), :, pl.ds(0, blocks)],
            dst.at[:, pl.ds(at, blocks)],
            sem.at[n],
        )
        if wait:
            cp.wait()
        else:
            cp.start()
        return 0

    lax.fori_loop(0, planes * NC, step, 0)


def line_up(off, src, dst, z, sign, planes, tail):
    width = GROUP + 128
    lane = lax.broadcasted_iota(jnp.int32, (8, width), 1)
    sub = lax.broadcasted_iota(jnp.int32, (8, 128), 0)

    def step(n, _):
        to = off[n] * BR
        at = pl.multiple_of((to // 128) * 128, 128)
        new = src[z + sign * (n // NC), lax.rem(n, NC)]
        new = pltpu.roll(jnp.concatenate([new, jnp.zeros((8, 128), jnp.float32)], axis=1), to - at, 1)
        old = dst[:, pl.ds(at, width)]
        dst[:, pl.ds(at, width)] = jnp.where(lane >= to - at, new, old)
        return 0

    lax.fori_loop(0, planes * NC, step, 0)
    total = off[planes * NC] * BR
    blank = jnp.where(sub == 0, tail, 0.0)
    for t in range(T // 128 + 1):
        at = pl.multiple_of((total // 128 + t) * 128, 128)
        old = dst[:, pl.ds(at, 128)]
        dst[:, pl.ds(at, 128)] = jnp.where(at + lane[:, :128] >= total, blank, old)


def backward_kernel(
    counts_hbm, qg, kv, st, info, stcol, dq_in, dkv_in, grads,
    counts, koff, qoff, kvc, qgc, stv, infov, qrow, krow, col, dqa, dka, dva, res, dkv, begin,
    csem, ksem, qsem, ssem, osem,
):
    z, x, core, _ = place()
    cp = pltpu.make_async_copy(counts_hbm, counts, csem)
    cp.start()
    smalls = [
        pltpu.make_async_copy(src, dst, ssem.at[i])
        for i, (src, dst) in enumerate(((st, stv), (info, infov), (stcol, col)))
    ]
    for small in smalls:
        small.start()
    cp.wait()
    top = z == NZ - 1
    early = pltpu.make_async_copy(dq_in, res.at[:, 0], osem.at[0])

    @pl.when(z < NZ - 1)
    def _():
        early.start()

    dkv_copy = pltpu.make_async_copy(dkv_in, dkv, osem.at[2])

    @pl.when(z == 0)
    def _():
        dkv_copy.start()

    @pl.when(z > 0)
    def _():
        def clear(j, _):
            for part in range(2):
                dkv[part, pl.ds(pl.multiple_of(j * SEG, SEG), SEG), :] = jnp.zeros((SEG, HD), jnp.float32)
            return 0

        lax.fori_loop(0, NS, clear, 0)

    zq = jnp.where(z == 0, NZ - 1, z)
    kplanes, qplanes = jnp.where(top, NZ, 1), NZ - zq
    fill_offsets(counts, koff, z, -1, kplanes)
    load(koff, kv, kvc, ksem, z, -1, kplanes, False)
    fill_offsets(counts, qoff, zq, 1, qplanes)
    load(qoff, qg, qgc, qsem, zq, 1, qplanes, False)
    key_end = koff[kplanes * NC]
    query_end = qoff[qplanes * NC]
    plane_end = jnp.where(z == 0, 0, koff[NC])
    zero = jnp.zeros((GROUP // BR, BR, HD), jnp.bfloat16)
    for part in range(2):
        kvc[part, pl.ds(key_end, GROUP // BR)] = zero
        qgc[part, pl.ds(query_end, GROUP // BR)] = zero
    for small in smalls:
        small.wait()
    line_up(koff, infov, krow, z, -1, kplanes, -FAR)
    line_up(qoff, stv, qrow, zq, 1, qplanes, FAR)
    base = koff[core]
    total = koff[core + 1] - base
    starts = [jnp.int32(0)]
    for j in range(NS):
        starts.append(starts[-1] + live_blocks(counts, z, core, j))
        begin[j] = starts[j]
    load(koff, kv, kvc, ksem, z, -1, kplanes, True)
    load(qoff, qg, qgc, qsem, zq, 1, qplanes, True)

    def tile(buf, part, t):
        return buf[part, pl.ds(t * (T // BR), T // BR)].reshape(T, HD)

    def run(M):
        rows = pl.ds(base, M // BR)
        r = lax.broadcasted_iota(jnp.int32, (M, 1), 0)
        start = jnp.zeros_like(r)
        shift = jnp.zeros_like(r) + lax.rem(core, NC) * BR
        for j in range(1, NS):
            inside = r >= starts[j] * BR
            start = jnp.where(inside, starts[j] * BR, start)
            shift = jnp.where(inside, j * CAP + lax.rem(core + j, NC) * BR, shift)
        t = r - start
        pos = (t + (t // BR) * BR + shift + z * (NS * CAP)).astype(jnp.float32)

        dka[0:M, :] = jnp.zeros((M, HD), jnp.float32)
        dva[0:M, :] = jnp.zeros((M, HD), jnp.float32)
        dqa[0:M, :] = jnp.zeros((M, HD), jnp.float32)

        def key_step(qt, _):
            lanes = pl.ds(pl.multiple_of(qt * T, T), T)
            qb, gb = tile(qgc, 0, qt), tile(qgc, 1, qt)
            p = jnp.exp2(dot(kvc[0, rows].reshape(M, HD), qb, NT) * SCALE2 - qrow[0:1, lanes])
            n = qt * T + lax.broadcasted_iota(jnp.int32, (1, T), 1)
            there = jnp.where(n < plane_end * BR, krow[1:2, lanes], FAR)
            p = jnp.where(pos <= there, p, 0.0)
            dva[0:M, :] += dot(p.astype(jnp.bfloat16), gb, NN)
            dp = dot(kvc[1, rows].reshape(M, HD), gb, NT)
            ds = (p * (dp - qrow[1:2, lanes])).astype(jnp.bfloat16)
            dka[0:M, :] += dot(ds, qb, NN)
            return 0

        def query_step(kt, _):
            lanes = pl.ds(pl.multiple_of(kt * T, T), T)
            kb, vb = tile(kvc, 0, kt), tile(kvc, 1, kt)
            s = dot(qgc[0, rows].reshape(M, HD), kb, NT) * SCALE2 + krow[0:1, lanes]
            s = jnp.where(krow[1:2, lanes] <= pos, s, -FAR)
            p = jnp.exp2(s - col[0:M, 0:1])
            dp = dot(qgc[1, rows].reshape(M, HD), vb, NT)
            dqa[0:M, :] += dot((p * (dp - col[0:M, 1:2])).astype(jnp.bfloat16), kb, NN)
            return 0

        per = T // BR
        lax.fori_loop(0, (query_end + per - 1) // per, key_step, 0)
        lax.fori_loop(0, jnp.where(top, (key_end + per - 1) // per, 0), query_step, 0)

    lower = 0
    for size in SIZES:

        @pl.when((total * BR > lower) & (total * BR <= size))
        def _():
            run(size)

        lower = size

    r = lax.broadcasted_iota(jnp.int32, (SEG, HD), 0)

    def spread(a, src, scale, more):
        def step(j, _):
            row = r + (r // BR + lax.rem(core + j, NC)) * BR
            part = src[pl.ds(pl.multiple_of(begin[j] * BR, BR), SEG), :]
            if more is not None:
                part = part + dkv[more, pl.ds(pl.multiple_of(j * SEG, SEG), SEG), :]
            part = jnp.where(row < counts[z * NS + j], part * scale, 0.0)
            res[j, a] = part.astype(jnp.bfloat16).reshape(SB, BR, HD)
            return 0

        lax.fori_loop(0, NS, step, 0)

    @pl.when(z == 0)
    def _():
        dkv_copy.wait()

    spread(1, dka, SCALE, 0)
    spread(2, dva, 1.0, 1)

    @pl.when(top)
    def _():
        spread(0, dqa, SCALE, None)

    @pl.when(z < NZ - 1)
    def _():
        early.wait()

    store = pltpu.make_async_copy(res, grads, osem.at[1])
    store.start()
    store.wait()


def backward(counts, qg, kv, st, info, stcol, dq, dkv):
    dma = pltpu.SemaphoreType.DMA
    blocks = (KEYS + GROUP + T) // BR
    return pl.pallas_call(
        backward_kernel,
        out_shape=GRADS,
        in_specs=[HBM] * 8,
        out_specs=HBM,
        scratch_shapes=[
            pltpu.SMEM((NZ * NS,), jnp.int32),
            pltpu.SMEM((NZ * NC + 1,), jnp.int32),
            pltpu.SMEM((NZ * NC + 1,), jnp.int32),
            pltpu.VMEM((2, blocks, BR, HD), jnp.bfloat16),
            pltpu.VMEM((2, blocks, BR, HD), jnp.bfloat16),
            pltpu.VMEM(ROWS, jnp.float32),
            pltpu.VMEM(ROWS, jnp.float32),
            pltpu.VMEM((8, KEYS + GROUP + T), jnp.float32),
            pltpu.VMEM((8, KEYS + GROUP + T), jnp.float32),
            pltpu.VMEM((GROUP, HD), jnp.float32),
            pltpu.VMEM((GROUP + SEG, HD), jnp.float32),
            pltpu.VMEM((GROUP + SEG, HD), jnp.float32),
            pltpu.VMEM((GROUP + SEG, HD), jnp.float32),
            pltpu.VMEM(GRADS.shape, jnp.bfloat16),
            pltpu.VMEM((2, GROUP, HD), jnp.float32),
            pltpu.SMEM((NS,), jnp.int32),
            dma,
            dma((NZ * NC,)),
            dma((NZ * NC,)),
            dma((3,)),
            dma((3,)),
        ],
        compiler_params=pltpu.CompilerParams(vmem_limit_bytes=VMEM_BYTES),
        name="backward",
    )(counts, qg, kv, st, info, stcol, dq, dkv)


def on_device(query_heads, key_heads, value_heads, grad_heads, counts):
    def blocks(array):
        return array.reshape(SB, 2, BR, NX * HD)

    kv, qg, att, st, info, stcol, dq, dkv = attend(
        blocks(query_heads), blocks(key_heads), blocks(value_heads), blocks(grad_heads), counts
    )
    grads = backward(counts, qg, kv, st, info, stcol, dq, dkv)
    return tuple(assemble(att, return_heads(grads)))


def solution(mesh):
    return jax.shard_map(
        on_device,
        mesh=mesh,
        in_specs=(P("ctx", "tp"), P("ctx", "tp"), P("ctx", "tp"), P("ctx", "tp"), P()),
        out_specs=(P("ctx", "tp"), P("ctx", "tp"), P("ctx", "tp"), P("ctx", "tp")),
        check_vma=False,
    )
```

```python
import functools

import jax
import jax.numpy as jnp
from jax import lax
from jax.experimental import pallas as pl
from jax.experimental.pallas import tpu as pltpu
from jax.sharding import PartitionSpec as P

HD = 128
NZ, NX, NC = 4, 4, 2
NS = NX * NC
BR = 16
SB = 8
SEG = SB * BR
CAP = 2 * SEG
GROUP = NS * SEG
KEYS = NZ * NC * GROUP
UNIT = NC * 2 * SEG
T = 512
SIZES = (640, 768, 1024)
FAR = 1e30
BIG = 1 << 30
SCALE = HD ** (-0.5)
SCALE2 = SCALE * 1.4426950408889634
MESH = pl.DeviceIdType.MESH
VMEM_BYTES = 56 * 1024 * 1024
SMEM = pl.BlockSpec(memory_space=pltpu.SMEM)
VMEM = pl.BlockSpec(memory_space=pltpu.VMEM)
HBM = pl.BlockSpec(memory_space=pltpu.HBM)
NT = (((1,), (1,)), ((), ()))
NN = (((1,), (0,)), ((), ()))


def dot(a, b, dims):
    return lax.dot_general(a, b, dims, preferred_element_type=jnp.float32)


def place():
    me = lax.axis_index("ctx")
    tp = lax.axis_index("tp")
    return me // (NC * NX), lax.rem(me // NC, NX), lax.rem(me, NC), tp


def ctx_of(z, x, core):
    return (z * NX + x) * NC + core


def cols(i):
    return pl.ds(pl.multiple_of(i * HD, HD), HD)


def remote(src, dst, ssem, rsem, dev):
    return pltpu.make_async_remote_copy(
        src_ref=src, dst_ref=dst, send_sem=ssem, recv_sem=rsem, device_id=dev, device_id_type=MESH
    )


def live_blocks(counts, p, c, j):
    nb = (counts[p * NS + j] + BR - 1) // BR
    return (nb + 1 - lax.rem(c + j, NC)) // 2


def attend_kernel(
    q, k, v, g, counts_hbm,
    kv_out, qg_out, att, st_out, info_out, col_out, dq_out, dkv_out,
    kvs, qgs, stage, dqs, dkv, kvp, qgp, stv, info, col, oc, m_ref, l_ref, acc, qpos_ref, counts, table,
    csem, loc, sa, ra, sown, sso, rso, sfw, ssf, rz, rs, sst, rst, sat, rat, lat, okv, oqg, ost, sdq, sdkv,
):
    z, x, core, tp = place()
    here = x * NC + core
    sib = (ctx_of(z, x, 1 - core), tp)
    above = (ctx_of(lax.rem(z + 1, NZ), x, core), tp)
    below = (ctx_of(lax.rem(z + NZ - 1, NZ), x, core), tp)
    has_up = z < NZ - 1
    has_dn = z > 0
    counts_copy = pltpu.make_async_copy(counts_hbm, counts, csem)
    counts_copy.start()
    partners = [(dx, dc) for dx in (0, 1, 3, 2) for dc in range(NC) if dx + dc > 0]

    def mate(dx, dc):
        return lax.rem(x + dx, NX), lax.rem(core + dc, NC)

    srcs = ((k, kvs, 0), (v, kvs, 1), (q, qgs, 0), (g, qgs, 1))
    own_parity = lax.rem(core + here, NC)
    own = []
    for a, (src, dst, part) in enumerate(srcs):
        cp = pltpu.make_async_copy(src.at[:, own_parity, :, cols(x)], dst.at[z, core, here, part], loc.at[a])
        cp.start()
        own.append(cp)

    barrier = pltpu.get_barrier_semaphore()
    for dx, dc in partners:
        px, pc = mate(dx, dc)
        pl.semaphore_signal(barrier, inc=1, device_id=(ctx_of(z, px, pc), tp), device_id_type=MESH)
    for dz in range(1, NZ):
        for pc in range(NC):
            pl.semaphore_signal(
                barrier, inc=1, device_id=(ctx_of(lax.rem(z + dz, NZ), x, pc), tp), device_id_type=MESH
            )
    pl.semaphore_wait(barrier, len(partners) + (NZ - 1) * NC)

    sends = []
    for dx, dc in partners:
        px, pc = mate(dx, dc)
        parity = lax.rem(pc + here, NC)
        for a, (src, dst, part) in enumerate(srcs):
            cp = remote(
                src.at[:, parity, :, cols(px)],
                dst.at[z, pc, here, part],
                sa.at[a, dx, dc],
                ra.at[a, dx, dc],
                (ctx_of(z, px, pc), tp),
            )
            cp.start()
            sends.append(cp)

    lane = lax.broadcasted_iota(jnp.int32, (8, SEG), 1)
    for j in range(NS):
        inside = (2 * (lane // BR) + lax.rem(core + j, NC)) * BR + lax.rem(lane, BR)
        qpos_ref[:, j * SEG : (j + 1) * SEG] = (z * NS + j) * CAP + inside
    m_ref[...] = jnp.full(m_ref.shape, -FAR, jnp.float32)
    l_ref[...] = jnp.zeros_like(l_ref)
    acc[...] = jnp.zeros_like(acc)
    dkv[...] = jnp.zeros_like(dkv)
    counts_copy.wait()
    wide_lane = lax.broadcasted_iota(jnp.int32, (8, GROUP), 1)
    wide_sub = lax.broadcasted_iota(jnp.int32, (8, GROUP), 0)

    def begins(p, c):
        at = [jnp.int32(0)]
        for j in range(NS):
            at.append(at[-1] + live_blocks(counts, p, c, j))
        return at

    def describe(n, _):
        p, c = n // NC, lax.rem(n, NC)
        at = begins(p, c)

        def source(b, _):
            shift = jnp.int32(0)
            for j in range(1, NS):
                shift = jnp.where(b >= at[j], j * SB - at[j], shift)
            table[n * (GROUP // BR) + b] = jnp.minimum(b + shift, GROUP // BR - 1)
            return 0

        lax.fori_loop(0, GROUP // BR, source, 0)
        start = jnp.zeros_like(wide_lane)
        shift = jnp.zeros_like(wide_lane) + c * BR
        kept = jnp.zeros_like(wide_lane) + counts[p * NS]
        for j in range(1, NS):
            inside = wide_lane >= at[j] * BR
            start = jnp.where(inside, at[j] * BR, start)
            shift = jnp.where(inside, j * CAP + lax.rem(c + j, NC) * BR, shift)
            kept = jnp.where(inside, j * CAP + counts[p * NS + j], kept)
        t = wide_lane - start
        pos = t + (t // BR) * BR + shift
        bias = jnp.where(pos < kept, 0.0, -FAR)
        info[p, c] = jnp.where(wide_sub == 0, bias, (pos + p * (NS * CAP)).astype(jnp.float32))
        return 0


    def pack(buf, dst, p):
        def group(c, _):
            stage[...] = buf[p, c]

            def step(i, _):
                for b in range(8):
                    n = table[(p * NC + c) * (GROUP // BR) + i * 8 + b]
                    j, r = n // SB, lax.rem(n, SB)
                    for part in range(2):
                        dst[p, c, part, i * 8 + b] = stage[j, part, r]
                return 0

            lax.fori_loop(0, GROUP // BR // 8, step, 0)
            return 0

        lax.fori_loop(0, NC, group, 0)

    def chunk(buf, p, c, xs):
        return buf.at[p, c, pl.ds(2 * xs, 2)]

    def keys_of(p, xs):
        inner = lax.broadcasted_iota(jnp.int32, (SEG, 1), 0)
        ks, vs, keys = [], [], []
        for c in range(NC):
            both = kvs[p, c, pl.ds(2 * xs, 2)]
            ks.append(both[:, 0].reshape(2 * SEG, HD))
            vs.append(both[:, 1].reshape(2 * SEG, HD))
            for jj in range(2):
                inside = (2 * (inner // BR) + (c + jj) % 2) * BR + lax.rem(inner, BR)
                live = inside < counts[p * NS + 2 * xs + jj]
                keys.append(jnp.where(live, (p * NS + 2 * xs + jj) * CAP + inside, BIG))
        kk = jnp.concatenate(ks, axis=0)
        vv = jnp.concatenate(vs, axis=0)
        s = dot(kk, qgs[z, core, :, 0].reshape(GROUP, HD), NT) * SCALE2
        return kk, vv, jnp.where(jnp.concatenate(keys, axis=0) <= qpos_ref[0:1, :], s, -FAR)

    def unit(p, xs):
        _, vv, s = keys_of(p, xs)
        m = m_ref[0:1, :]
        new = jnp.maximum(m, jnp.max(s, axis=0, keepdims=True))
        pr = jnp.exp2(s - new)
        f = jnp.exp2(m - new)
        m_ref[0:1, :] = new
        l_ref[0:1, :] = l_ref[0:1, :] * f + jnp.sum(pr, axis=0, keepdims=True)
        acc[...] = acc[...] * f + dot(vv.T, pr.astype(jnp.bfloat16), NN)

    def unit_back(p, xs):
        kk, vv, s = keys_of(p, xs)
        pr = jnp.exp2(s - m_ref[0:1, :])
        dp = dot(vv, qgs[z, core, :, 1].reshape(GROUP, HD), NT)
        ds = (pr * (dp - l_ref[0:1, :])).astype(jnp.bfloat16)
        acc[...] += dot(kk.T, ds, NN)

    def unit_key(p, xs):
        line = lax.broadcasted_iota(jnp.int32, (1, SEG), 1)
        inner = lax.broadcasted_iota(jnp.int32, (SEG, 1), 0)
        qs, gs, lses, deltas, queries, keys = [], [], [], [], [], []
        for c in range(NC):
            both = qgs[p, c, pl.ds(2 * xs, 2)]
            qs.append(both[:, 0].reshape(2 * SEG, HD))
            gs.append(both[:, 1].reshape(2 * SEG, HD))
            lanes = pl.ds(pl.multiple_of(2 * xs * SEG, 2 * SEG), 2 * SEG)
            lses.append(stv[p, c, 2:3, lanes])
            deltas.append(stv[p, c, 3:4, lanes])
            for jj in range(2):
                inside = (2 * (line // BR) + (c + jj) % 2) * BR + lax.rem(line, BR)
                queries.append((p * NS + 2 * xs + jj) * CAP + inside)
        for j in range(NS):
            keys.append((z * NS + j) * CAP + (2 * (inner // BR) + lax.rem(core + j, NC)) * BR + lax.rem(inner, BR))
        qq, gg = jnp.concatenate(qs, axis=0), jnp.concatenate(gs, axis=0)
        lse, delta = jnp.concatenate(lses, axis=1), jnp.concatenate(deltas, axis=1)
        s = dot(kvs[z, core, :, 0].reshape(GROUP, HD), qq, NT) * SCALE2
        pr = jnp.exp2(s - lse)
        pr = jnp.where(jnp.concatenate(keys, axis=0) <= jnp.concatenate(queries, axis=1), pr, 0.0)
        dkv[1] += dot(pr.astype(jnp.bfloat16), gg, NN)
        dp = dot(kvs[z, core, :, 1].reshape(GROUP, HD), gg, NT)
        dkv[0] += dot((pr * (dp - delta)).astype(jnp.bfloat16), qq, NN)

    flows = ((kvs, -1, has_up, above), (qgs, 1, has_dn, below))

    def place_of(t):
        m = lax.rem(t, NX)
        return t // NX, m, lax.rem(x + NX - (m + m // 2 - 2 * (m // 3)), NX)

    def own_comm(m):
        _, _, xs = place_of(m)
        dx = lax.rem(x + NX - xs, NX)
        for half, (buf, _, has, dev) in enumerate(flows):
            for part in range(2):
                a = 2 * half + part
                for dc in range(NC):
                    ref = buf.at[z, core, xs * NC + lax.rem(core + dc, NC), part]
                    if dc == 0:

                        @pl.when(m == 0)
                        def _():
                            own[a].wait()

                        @pl.when(m > 0)
                        def _():
                            remote(ref, ref, sa.at[a, dx, dc], ra.at[a, dx, dc], sib).wait_recv()

                    else:
                        remote(ref, ref, sa.at[a, dx, dc], ra.at[a, dx, dc], sib).wait_recv()
            ref = chunk(buf, z, core, xs)

            @pl.when(has)
            def _():
                remote(ref, ref, sown.at[half, m], rz.at[z, m], dev).start()

            remote(ref, ref, sso.at[half, m], rso.at[half, m], sib).start()

    def comm(t):
        d, m, xs = place_of(t)
        for buf, sign, has, dev in flows:
            p = z + sign * (d + 1)

            @pl.when((p >= 0) & (p < NZ))
            def _():
                ref = chunk(buf, p, core, xs)
                remote(ref, ref, sfw.at[p, m], rz.at[p, m], sib).wait_recv()

                @pl.when(has)
                def _():
                    remote(ref, ref, sfw.at[p, m], rz.at[p, m], dev).start()

                remote(ref, ref, ssf.at[p, m], rs.at[p, m], sib).start()

    def work(u, _):
        d, m, xs = place_of(u)

        @pl.when(d == 0)
        def _():
            for half, (buf, _, has, dev) in enumerate(flows):
                ref = chunk(buf, z, 1 - core, xs)
                remote(ref, ref, sso.at[half, m], rso.at[half, m], sib).wait_recv()

        for buf, sign, has, dev in flows:
            p = z + sign * d

            @pl.when((d > 0) & (p >= 0) & (p < NZ))
            def _():
                ref = chunk(buf, p, 1 - core, xs)
                remote(ref, ref, ssf.at[p, m], rs.at[p, m], sib).wait_recv()

        @pl.when(z - d >= 0)
        def _():
            unit(z - d, xs)

        whole = (m == NX - 1) & (d < NZ - 1)

        @pl.when(whole & ((d == 0) | (z == NZ - 1)))
        def _():
            pack(kvs, kvp, z - d)

        @pl.when(whole & (z + d < NZ) & ((z > 1) | (z + d == NZ - 1)))
        def _():
            pack(qgs, qgp, z + d)

        return 0

    def own_step(m, _):
        own_comm(m)
        describe(2 * m, 0)
        describe(2 * m + 1, 0)
        return 0

    stats = stv.at[z, core]

    def send_stats(act):
        act(remote(stats, stats, sst.at[0], rst.at[z, core], sib))
        for dz in range(1, NZ):

            @pl.when(z - dz >= 0)
            def _():
                for pc in range(NC):
                    dev = (ctx_of(z - dz, x, pc), tp)
                    act(remote(stats, stats, sst.at[dz * NC + pc], rst.at[z, core], dev))

    def send_rows(act):
        for dx, dc in partners:
            px, pc = mate(dx, dc)
            there = px * NC + pc
            parity = lax.rem(core + there, NC)
            act(
                remote(
                    oc.at[there], att.at[x, :, parity], sat.at[dx, dc], rat.at[dx, dc], (ctx_of(z, px, pc), tp)
                )
            )

    stay = pltpu.make_async_copy(oc.at[here], att.at[x, :, own_parity], lat)

    def finish():
        sub = lax.broadcasted_iota(jnp.int32, (8, SEG), 0)
        at = begins(z, core)
        packed = jnp.where(wide_sub == 0, FAR, 0.0)
        for j in range(NS):
            rows = slice(j * SEG, (j + 1) * SEG)
            live = qpos_ref[0:1, rows] - (z * NS + j) * CAP < counts[z * NS + j]
            l = l_ref[0:1, rows]
            o = jnp.where(live, acc[:, rows] / l, 0.0).T.astype(jnp.bfloat16)
            oc[j] = o.reshape(SB, BR, HD)
            cot = qgs[z, core, j, 1].reshape(SEG, HD).astype(jnp.float32)
            delta = jnp.sum(o.astype(jnp.float32) * cot, axis=1, keepdims=True)
            lse = jnp.where(live, m_ref[0:1, rows] + jnp.log2(l), FAR)
            both = jnp.where(sub == 0, lse, jnp.broadcast_to(delta, (SEG, HD)).T[:8, :])
            m_ref[0:1, rows] = lse
            l_ref[0:1, rows] = both[1:2, :]
            both = jnp.concatenate([both, jnp.zeros((8, GROUP - SEG), jnp.float32)], axis=1)
            inside = (wide_lane >= at[j] * BR) & (wide_lane < at[j + 1] * BR)
            packed = jnp.where(inside, pltpu.roll(both, at[j] * BR, 1), packed)
        dense = jnp.where(wide_sub == 2, m_ref[0:1, :], l_ref[0:1, :])
        stv[z, core] = jnp.where(wide_sub < 2, packed, dense)
        for j in range(NS):
            rows = slice(j * SEG, (j + 1) * SEG)
            block = jnp.concatenate([packed[:, rows], jnp.zeros((SEG - 8, SEG), jnp.float32)], axis=0)
            col[rows, :] = block.T

        acc[...] = jnp.zeros_like(acc)
        send_stats(lambda cp: cp.start())
        send_rows(lambda cp: cp.start())
        stay.start()

    top = z == NZ - 1
    done = jnp.where(z == 0, 1, 4 * z)
    pace = jnp.where(z == NZ - 2, 3, jnp.where(z == 1, 2, 1))

    def back(u, _):
        d, m, xs = place_of(u)
        unit_back(z - d, xs)
        return 0

    def key_work(w, _):
        d, m, xs = place_of(w)
        p = z + d
        for c in range(NC):

            @pl.when((m == 0) & ((d > 0) | (c != core)))
            def _():
                ref = stv.at[p, c]
                remote(ref, ref, sst.at[0], rst.at[p, c], sib).wait_recv()

        unit_key(p, xs)
        return 0

    def step(t, _):
        @pl.when(t < (NZ - 1) * NX)
        def _():
            comm(t)

        lax.fori_loop(jnp.where(t < 3, 2 * t, t + 3), jnp.where(t < 3, 2 * t + 2, t + 4), work, 0)

        @pl.when(t == done)
        def _():
            finish()

        @pl.when((t > done) & (z < NZ - 1))
        def _():
            first = (t - done - 1) * pace
            last = jnp.maximum(first, jnp.minimum(first + pace, NX * (z + 1)))
            lax.fori_loop(first, last, back, 0)

        start = jnp.where(z == 0, 6, 9)

        @pl.when((z <= 1) & (t >= start) & (t < start + 2 * (NZ - 1 - z)))
        def _():
            lax.fori_loop(2 * (t - start), 2 * (t - start) + 2, key_work, 0)

        return 0

    lax.fori_loop(0, NX, own_step, 0)
    lax.fori_loop(0, (NZ - 1) * NX + 1, step, 0)

    @pl.when(z < NZ - 1)
    def _():
        for j in range(NS):
            rows = slice(j * SEG, (j + 1) * SEG)
            dqs[j] = (acc[:, rows] * SCALE).T.astype(jnp.bfloat16).reshape(SB, BR, HD)
        pltpu.make_async_copy(dqs, dq_out, sdq).start()

    @pl.when(z <= 1)
    def _():
        pltpu.make_async_copy(dkv, dkv_out, sdkv).start()

    @pl.when(z == NZ - 1)
    def _():
        pack(kvs, kvp, 0)

    @pl.when(z == 0)
    def _():
        pack(qgs, qgp, NZ - 1)

    outs = [
        pltpu.make_async_copy(col, col_out, ost.at[NZ, 0]),
        pltpu.make_async_copy(info, info_out, ost.at[NZ, 1]),
    ]
    for buf, dst, sem in ((kvp, kv_out, okv), (qgp, qg_out, oqg)):
        outs.append(pltpu.make_async_copy(buf.at[z], dst.at[z], sem.at[z]))
    for cp in outs:
        cp.start()
    def copies(act, take):
        for dz in range(1, NZ):

            @pl.when((z - dz >= 0) & (z == NZ - 1))
            def _():
                act(pltpu.make_async_copy(kvp.at[z - dz], kv_out.at[z - dz], okv.at[z - dz]))

            @pl.when((z + dz < NZ) & ((z > 1) | (z + dz == NZ - 1)))
            def _():
                act(pltpu.make_async_copy(qgp.at[z + dz], qg_out.at[z + dz], oqg.at[z + dz]))

        @pl.when(z > 1)
        def _():
            act(pltpu.make_async_copy(stats, st_out.at[z, core], ost.at[z, core]))
            take(z, 1 - core)

        for dz in range(1, NZ):

            @pl.when((z + dz < NZ) & ((z > 1) | (z + dz == NZ - 1)))
            def _():
                for c in range(NC):
                    take(z + dz, c)

    def take(p, c):
        ref = stv.at[p, c]
        remote(ref, ref, sst.at[0], rst.at[p, c], sib).wait_recv()
        pltpu.make_async_copy(ref, st_out.at[p, c], ost.at[p, c]).start()

    copies(lambda cp: cp.start(), take)

    for cp in outs:
        cp.wait()
    stay.wait()
    for dx, dc in partners:
        ox, oc_ = lax.rem(x + NX - dx, NX), lax.rem(core + NC - dc, NC)
        parity = lax.rem(oc_ + here, NC)
        ref = att.at[ox, :, parity]
        remote(oc.at[here], ref, sat.at[dx, dc], rat.at[dx, dc], sib).wait_recv()
    for cp in sends:
        cp.wait_send()
    send_rows(lambda cp: cp.wait_send())
    send_stats(lambda cp: cp.wait_send())

    @pl.when(z < NZ - 1)
    def _():
        pltpu.make_async_copy(dqs, dq_out, sdq).wait()

    @pl.when(z <= 1)
    def _():
        pltpu.make_async_copy(dkv, dkv_out, sdkv).wait()

    copies(
        lambda cp: cp.wait(),
        lambda p, c: pltpu.make_async_copy(stv.at[p, c], st_out.at[p, c], ost.at[p, c]).wait(),
    )

    for m in range(NX):
        _, _, xs = place_of(jnp.int32(m))
        for half, (buf, _, has, dev) in enumerate(flows):
            ref = chunk(buf, z, core, xs)

            @pl.when(has)
            def _():
                remote(ref, ref, sown.at[half, m], rz.at[z, m], dev).wait_send()

            remote(ref, ref, sso.at[half, m], rso.at[half, m], sib).wait_send()

    def sent(t, _):
        d, m, xs = place_of(t)
        for buf, sign, has, dev in flows:
            p = z + sign * (d + 1)

            @pl.when((p >= 0) & (p < NZ))
            def _():
                ref = chunk(buf, p, core, xs)

                @pl.when(has)
                def _():
                    remote(ref, ref, sfw.at[p, m], rz.at[p, m], dev).wait_send()

                remote(ref, ref, ssf.at[p, m], rs.at[p, m], sib).wait_send()

        return 0

    lax.fori_loop(0, (NZ - 1) * NX, sent, 0)


WHOLE = (NZ, NC, NS, 2, SB, BR, HD)
PACKED = (NZ, NC, 2, GROUP // BR, BR, HD)
ROWS = (NZ, NC, 8, GROUP)
LANDED = jax.ShapeDtypeStruct((NX, SB, 2, BR, HD), jnp.bfloat16)
PARTS = jax.ShapeDtypeStruct((NS, SB, BR, HD), jnp.bfloat16)
GRADS = jax.ShapeDtypeStruct((NS, 3, SB, BR, HD), jnp.bfloat16)
LANDED3 = jax.ShapeDtypeStruct((NX, 3, SB, 2, BR, HD), jnp.bfloat16)


def attend(q, k, v, g, counts):
    dma = pltpu.SemaphoreType.DMA
    packed = jax.ShapeDtypeStruct(PACKED, jnp.bfloat16)
    rows = jax.ShapeDtypeStruct(ROWS, jnp.float32)
    return pl.pallas_call(
        attend_kernel,
        out_shape=(
            packed,
            packed,
            LANDED,
            rows,
            rows,
            jax.ShapeDtypeStruct((GROUP, HD), jnp.float32),
            PARTS,
            jax.ShapeDtypeStruct((2, GROUP, HD), jnp.float32),
        ),
        in_specs=[HBM] * 5,
        out_specs=(HBM,) * 8,
        scratch_shapes=[
            pltpu.VMEM(WHOLE, jnp.bfloat16),
            pltpu.VMEM(WHOLE, jnp.bfloat16),
            pltpu.VMEM((NS, 2, SB, BR, HD), jnp.bfloat16),
            pltpu.VMEM((NS, SB, BR, HD), jnp.bfloat16),
            pltpu.VMEM((2, GROUP, HD), jnp.float32),
            pltpu.VMEM(PACKED, jnp.bfloat16),
            pltpu.VMEM(PACKED, jnp.bfloat16),
            pltpu.VMEM(ROWS, jnp.float32),
            pltpu.VMEM(ROWS, jnp.float32),
            pltpu.VMEM((GROUP, HD), jnp.float32),
            pltpu.VMEM((NS, SB, BR, HD), jnp.bfloat16),
            pltpu.VMEM((8, GROUP), jnp.float32),
            pltpu.VMEM((8, GROUP), jnp.float32),
            pltpu.VMEM((HD, GROUP), jnp.float32),
            pltpu.VMEM((8, GROUP), jnp.int32),
            pltpu.SMEM((NZ * NS,), jnp.int32),
            pltpu.SMEM((NZ * NC * (GROUP // BR),), jnp.int32),
            dma,
            dma((4,)),
            dma((4, NX, NC)),
            dma((4, NX, NC)),
            dma((2, NX)),
            dma((2, NX)),
            dma((2, NX)),
            dma((NZ, NX)),
            dma((NZ, NX)),
            dma((NZ, NX)),
            dma((NZ, NX)),
            dma((NZ * NC,)),
            dma((NZ, NC)),
            dma((NX, NC)),
            dma((NX, NC)),
            dma,
            dma((NZ,)),
            dma((NZ,)),
            dma((NZ + 1, NC)),
            dma,
            dma,
        ],
        compiler_params=pltpu.CompilerParams(
            collective_id=0, has_side_effects=True, vmem_limit_bytes=VMEM_BYTES
        ),
        name="attend",
    )(q, k, v, g, counts)


def return_kernel(grads, out, loc, ssem, rsem):
    z, x, core, tp = place()
    here = x * NC + core
    partners = [(dx, dc) for dx in (2, 1, 3, 0) for dc in range(NC) if dx + dc > 0]
    own = pltpu.make_async_copy(grads.at[here], out.at[x, :, :, lax.rem(core + here, NC)], loc)
    own.start()
    barrier = pltpu.get_barrier_semaphore()
    for dx, dc in partners:
        dev = (ctx_of(z, lax.rem(x + dx, NX), lax.rem(core + dc, NC)), tp)
        pl.semaphore_signal(barrier, inc=1, device_id=dev, device_id_type=MESH)
    pl.semaphore_wait(barrier, len(partners))
    sends = []
    for dx, dc in partners:
        px, pc = lax.rem(x + dx, NX), lax.rem(core + dc, NC)
        there = px * NC + pc
        cp = remote(
            grads.at[there],
            out.at[x, :, :, lax.rem(core + there, NC)],
            ssem.at[dx, dc],
            rsem.at[dx, dc],
            (ctx_of(z, px, pc), tp),
        )
        cp.start()
        sends.append(cp)
    own.wait()
    for dx, dc in partners:
        ox, oc = lax.rem(x + NX - dx, NX), lax.rem(core + NC - dc, NC)
        ref = out.at[ox, :, :, lax.rem(oc + here, NC)]
        remote(grads.at[here], ref, ssem.at[dx, dc], rsem.at[dx, dc], (ctx_of(z, ox, oc), tp)).wait_recv()
    for cp in sends:
        cp.wait_send()


def return_heads(grads):
    dma = pltpu.SemaphoreType.DMA
    return pl.pallas_call(
        return_kernel,
        out_shape=LANDED3,
        in_specs=[HBM],
        out_specs=HBM,
        scratch_shapes=[dma, dma((NX, NC)), dma((NX, NC))],
        compiler_params=pltpu.CompilerParams(collective_id=1, has_side_effects=True),
        name="return_heads",
    )(grads)


def assemble_kernel(att, grads, *refs):
    outs = refs[:4]
    buf0, buf, res, lsem, ssem = refs[4:]
    loads = [pltpu.make_async_copy(att, buf0, lsem.at[0])]
    loads += [pltpu.make_async_copy(grads.at[:, a], buf.at[:, a], lsem.at[a + 1]) for a in range(3)]
    for cp in loads:
        cp.start()
    stores = [pltpu.make_async_copy(res.at[a], outs[a], ssem.at[a]) for a in range(4)]
    for a in range(4):
        loads[a].wait()
        for i in range(NX):
            part = buf0[i] if a == 0 else buf[i, a - 1]
            res[a, :, i * HD : (i + 1) * HD] = part.reshape(CAP, HD)
        stores[a].start()
    for cp in stores:
        cp.wait()


def assemble(att, grads):
    dma = pltpu.SemaphoreType.DMA
    shape = jax.ShapeDtypeStruct((CAP, NX * HD), jnp.bfloat16)
    return pl.pallas_call(
        assemble_kernel,
        out_shape=(shape,) * 4,
        in_specs=[HBM] * 2,
        out_specs=(HBM,) * 4,
        scratch_shapes=[
            pltpu.VMEM(LANDED.shape, jnp.bfloat16),
            pltpu.VMEM(LANDED3.shape, jnp.bfloat16),
            pltpu.VMEM((4, CAP, NX * HD), jnp.bfloat16),
            dma((4,)),
            dma((4,)),
        ],
        compiler_params=pltpu.CompilerParams(vmem_limit_bytes=VMEM_BYTES),
        name="assemble",
    )(att, grads)


def fill_offsets(counts, off, z, sign, planes):
    def step(n, at):
        off[n] = at
        p, c = z + sign * (n // NC), lax.rem(n, NC)
        for j in range(NS):
            at = at + live_blocks(counts, p, c, j)
        return at

    off[planes * NC] = lax.fori_loop(0, planes * NC, step, jnp.int32(0))


def load(off, src, dst, sem, z, sign, planes, wait):
    def step(n, _):
        at = off[n]
        blocks = off[n + 1] - at
        cp = pltpu.make_async_copy(
            src.at[z + sign * (n // NC), lax.rem(n, NC), :, pl.ds(0, blocks)],
            dst.at[:, pl.ds(at, blocks)],
            sem.at[n],
        )
        if wait:
            cp.wait()
        else:
            cp.start()
        return 0

    lax.fori_loop(0, planes * NC, step, 0)


def line_up(off, src, dst, z, sign, planes, tail):
    width = GROUP + 128
    lane = lax.broadcasted_iota(jnp.int32, (8, width), 1)
    sub = lax.broadcasted_iota(jnp.int32, (8, 128), 0)

    def step(n, _):
        to = off[n] * BR
        at = pl.multiple_of((to // 128) * 128, 128)
        new = src[z + sign * (n // NC), lax.rem(n, NC)]
        new = pltpu.roll(jnp.concatenate([new, jnp.zeros((8, 128), jnp.float32)], axis=1), to - at, 1)
        old = dst[:, pl.ds(at, width)]
        dst[:, pl.ds(at, width)] = jnp.where(lane >= to - at, new, old)
        return 0

    lax.fori_loop(0, planes * NC, step, 0)
    total = off[planes * NC] * BR
    blank = jnp.where(sub == 0, tail, 0.0)
    for t in range(T // 128 + 1):
        at = pl.multiple_of((total // 128 + t) * 128, 128)
        old = dst[:, pl.ds(at, 128)]
        dst[:, pl.ds(at, 128)] = jnp.where(at + lane[:, :128] >= total, blank, old)


def backward_kernel(
    counts_hbm, qg, kv, st, info, stcol, dq_in, dkv_in, grads,
    counts, koff, qoff, kvc, qgc, stv, infov, qrow, krow, col, dqa, dka, dva, res, dkv, begin,
    csem, ksem, qsem, ssem, osem,
):
    z, x, core, _ = place()
    cp = pltpu.make_async_copy(counts_hbm, counts, csem)
    cp.start()
    smalls = [
        pltpu.make_async_copy(src, dst, ssem.at[i])
        for i, (src, dst) in enumerate(((st, stv), (info, infov), (stcol, col)))
    ]
    for small in smalls:
        small.start()
    cp.wait()
    top = z == NZ - 1
    early = pltpu.make_async_copy(dq_in, res.at[:, 0], osem.at[0])

    @pl.when(z < NZ - 1)
    def _():
        early.start()

    dkv_copy = pltpu.make_async_copy(dkv_in, dkv, osem.at[2])

    @pl.when(z <= 1)
    def _():
        dkv_copy.start()

    @pl.when(z > 1)
    def _():
        def clear(j, _):
            for part in range(2):
                dkv[part, pl.ds(pl.multiple_of(j * SEG, SEG), SEG), :] = jnp.zeros((SEG, HD), jnp.float32)
            return 0

        lax.fori_loop(0, NS, clear, 0)

    zq = jnp.where(z <= 1, NZ - 1, z)
    kplanes, qplanes = jnp.where(top, NZ, 1), NZ - zq
    fill_offsets(counts, koff, z, -1, kplanes)
    load(koff, kv, kvc, ksem, z, -1, kplanes, False)
    fill_offsets(counts, qoff, zq, 1, qplanes)
    load(qoff, qg, qgc, qsem, zq, 1, qplanes, False)
    key_end = koff[kplanes * NC]
    query_end = qoff[qplanes * NC]
    plane_end = jnp.where(z <= 1, 0, koff[NC])
    zero = jnp.zeros((GROUP // BR, BR, HD), jnp.bfloat16)
    for part in range(2):
        kvc[part, pl.ds(key_end, GROUP // BR)] = zero
        qgc[part, pl.ds(query_end, GROUP // BR)] = zero
    for small in smalls:
        small.wait()
    line_up(koff, infov, krow, z, -1, kplanes, -FAR)
    line_up(qoff, stv, qrow, zq, 1, qplanes, FAR)
    base = koff[core]
    total = koff[core + 1] - base
    starts = [jnp.int32(0)]
    for j in range(NS):
        starts.append(starts[-1] + live_blocks(counts, z, core, j))
        begin[j] = starts[j]
    load(koff, kv, kvc, ksem, z, -1, kplanes, True)
    load(qoff, qg, qgc, qsem, zq, 1, qplanes, True)

    def tile(buf, part, t):
        return buf[part, pl.ds(t * (T // BR), T // BR)].reshape(T, HD)

    def run(M):
        rows = pl.ds(base, M // BR)
        r = lax.broadcasted_iota(jnp.int32, (M, 1), 0)
        start = jnp.zeros_like(r)
        shift = jnp.zeros_like(r) + lax.rem(core, NC) * BR
        for j in range(1, NS):
            inside = r >= starts[j] * BR
            start = jnp.where(inside, starts[j] * BR, start)
            shift = jnp.where(inside, j * CAP + lax.rem(core + j, NC) * BR, shift)
        t = r - start
        pos = (t + (t // BR) * BR + shift + z * (NS * CAP)).astype(jnp.float32)

        dka[0:M, :] = jnp.zeros((M, HD), jnp.float32)
        dva[0:M, :] = jnp.zeros((M, HD), jnp.float32)
        dqa[0:M, :] = jnp.zeros((M, HD), jnp.float32)

        def key_step(qt, _):
            lanes = pl.ds(pl.multiple_of(qt * T, T), T)
            qb, gb = tile(qgc, 0, qt), tile(qgc, 1, qt)
            p = jnp.exp2(dot(kvc[0, rows].reshape(M, HD), qb, NT) * SCALE2 - qrow[0:1, lanes])
            n = qt * T + lax.broadcasted_iota(jnp.int32, (1, T), 1)
            there = jnp.where(n < plane_end * BR, krow[1:2, lanes], FAR)
            p = jnp.where(pos <= there, p, 0.0)
            dva[0:M, :] += dot(p.astype(jnp.bfloat16), gb, NN)
            dp = dot(kvc[1, rows].reshape(M, HD), gb, NT)
            ds = (p * (dp - qrow[1:2, lanes])).astype(jnp.bfloat16)
            dka[0:M, :] += dot(ds, qb, NN)
            return 0

        def query_step(kt, _):
            lanes = pl.ds(pl.multiple_of(kt * T, T), T)
            kb, vb = tile(kvc, 0, kt), tile(kvc, 1, kt)
            s = dot(qgc[0, rows].reshape(M, HD), kb, NT) * SCALE2 + krow[0:1, lanes]
            s = jnp.where(krow[1:2, lanes] <= pos, s, -FAR)
            p = jnp.exp2(s - col[0:M, 0:1])
            dp = dot(qgc[1, rows].reshape(M, HD), vb, NT)
            dqa[0:M, :] += dot((p * (dp - col[0:M, 1:2])).astype(jnp.bfloat16), kb, NN)
            return 0

        per = T // BR
        lax.fori_loop(0, (query_end + per - 1) // per, key_step, 0)
        lax.fori_loop(0, jnp.where(top, (key_end + per - 1) // per, 0), query_step, 0)

    lower = 0
    for size in SIZES:

        @pl.when((total * BR > lower) & (total * BR <= size))
        def _():
            run(size)

        lower = size

    r = lax.broadcasted_iota(jnp.int32, (SEG, HD), 0)

    def spread(a, src, scale, more):
        def step(j, _):
            row = r + (r // BR + lax.rem(core + j, NC)) * BR
            part = src[pl.ds(pl.multiple_of(begin[j] * BR, BR), SEG), :]
            if more is not None:
                part = part + dkv[more, pl.ds(pl.multiple_of(j * SEG, SEG), SEG), :]
            part = jnp.where(row < counts[z * NS + j], part * scale, 0.0)
            res[j, a] = part.astype(jnp.bfloat16).reshape(SB, BR, HD)
            return 0

        lax.fori_loop(0, NS, step, 0)

    @pl.when(z <= 1)
    def _():
        dkv_copy.wait()

    spread(1, dka, SCALE, 0)
    spread(2, dva, 1.0, 1)

    @pl.when(top)
    def _():
        spread(0, dqa, SCALE, None)

    @pl.when(z < NZ - 1)
    def _():
        early.wait()

    store = pltpu.make_async_copy(res, grads, osem.at[1])
    store.start()
    store.wait()


def backward(counts, qg, kv, st, info, stcol, dq, dkv):
    dma = pltpu.SemaphoreType.DMA
    blocks = (KEYS + GROUP + T) // BR
    return pl.pallas_call(
        backward_kernel,
        out_shape=GRADS,
        in_specs=[HBM] * 8,
        out_specs=HBM,
        scratch_shapes=[
            pltpu.SMEM((NZ * NS,), jnp.int32),
            pltpu.SMEM((NZ * NC + 1,), jnp.int32),
            pltpu.SMEM((NZ * NC + 1,), jnp.int32),
            pltpu.VMEM((2, blocks, BR, HD), jnp.bfloat16),
            pltpu.VMEM((2, blocks, BR, HD), jnp.bfloat16),
            pltpu.VMEM(ROWS, jnp.float32),
            pltpu.VMEM(ROWS, jnp.float32),
            pltpu.VMEM((8, KEYS + GROUP + T), jnp.float32),
            pltpu.VMEM((8, KEYS + GROUP + T), jnp.float32),
            pltpu.VMEM((GROUP, HD), jnp.float32),
            pltpu.VMEM((GROUP + SEG, HD), jnp.float32),
            pltpu.VMEM((GROUP + SEG, HD), jnp.float32),
            pltpu.VMEM((GROUP + SEG, HD), jnp.float32),
            pltpu.VMEM(GRADS.shape, jnp.bfloat16),
            pltpu.VMEM((2, GROUP, HD), jnp.float32),
            pltpu.SMEM((NS,), jnp.int32),
            dma,
            dma((NZ * NC,)),
            dma((NZ * NC,)),
            dma((3,)),
            dma((3,)),
        ],
        compiler_params=pltpu.CompilerParams(vmem_limit_bytes=VMEM_BYTES),
        name="backward",
    )(counts, qg, kv, st, info, stcol, dq, dkv)


def on_device(query_heads, key_heads, value_heads, grad_heads, counts):
    def blocks(array):
        return array.reshape(SB, 2, BR, NX * HD)

    kv, qg, att, st, info, stcol, dq, dkv = attend(
        blocks(query_heads), blocks(key_heads), blocks(value_heads), blocks(grad_heads), counts
    )
    grads = backward(counts, qg, kv, st, info, stcol, dq, dkv)
    return tuple(assemble(att, return_heads(grads)))


def solution(mesh):
    return jax.shard_map(
        on_device,
        mesh=mesh,
        in_specs=(P("ctx", "tp"), P("ctx", "tp"), P("ctx", "tp"), P("ctx", "tp"), P()),
        out_specs=(P("ctx", "tp"), P("ctx", "tp"), P("ctx", "tp"), P("ctx", "tp")),
        check_vma=False,
    )
```

```python
import functools

import jax
import jax.numpy as jnp
from jax import lax
from jax.experimental import pallas as pl
from jax.experimental.pallas import tpu as pltpu
from jax.sharding import PartitionSpec as P

HD = 128
NZ, NX, NC = 4, 4, 2
NS = NX * NC
BR = 16
SB = 8
SEG = SB * BR
CAP = 2 * SEG
GROUP = NS * SEG
KEYS = NZ * NC * GROUP
UNIT = NC * 2 * SEG
T = 512
SIZES = (640, 768, 1024)
FAR = 1e30
BIG = 1 << 30
SCALE = HD ** (-0.5)
SCALE2 = SCALE * 1.4426950408889634
MESH = pl.DeviceIdType.MESH
VMEM_BYTES = 56 * 1024 * 1024
SMEM = pl.BlockSpec(memory_space=pltpu.SMEM)
VMEM = pl.BlockSpec(memory_space=pltpu.VMEM)
HBM = pl.BlockSpec(memory_space=pltpu.HBM)
NT = (((1,), (1,)), ((), ()))
NN = (((1,), (0,)), ((), ()))


def dot(a, b, dims):
    return lax.dot_general(a, b, dims, preferred_element_type=jnp.float32)


def place():
    me = lax.axis_index("ctx")
    tp = lax.axis_index("tp")
    return me // (NC * NX), lax.rem(me // NC, NX), lax.rem(me, NC), tp


def ctx_of(z, x, core):
    return (z * NX + x) * NC + core


def cols(i):
    return pl.ds(pl.multiple_of(i * HD, HD), HD)


def remote(src, dst, ssem, rsem, dev):
    return pltpu.make_async_remote_copy(
        src_ref=src, dst_ref=dst, send_sem=ssem, recv_sem=rsem, device_id=dev, device_id_type=MESH
    )


def live_blocks(counts, p, c, j):
    nb = (counts[p * NS + j] + BR - 1) // BR
    return (nb + 1 - lax.rem(c + j, NC)) // 2


def attend_kernel(
    q, k, v, g, counts_hbm,
    kv_out, qg_out, att, st_out, info_out, col_out, dq_out, dkv_out,
    kvs, qgs, stage, dqs, dkv, kvp, qgp, stv, info, col, oc, m_ref, l_ref, acc, qpos_ref, counts, table,
    csem, loc, sa, ra, sown, sso, rso, sfw, ssf, rz, rs, sst, rst, sat, rat, lat, okv, oqg, ost, sdq, sdkv,
):
    z, x, core, tp = place()
    here = x * NC + core
    sib = (ctx_of(z, x, 1 - core), tp)
    above = (ctx_of(lax.rem(z + 1, NZ), x, core), tp)
    below = (ctx_of(lax.rem(z + NZ - 1, NZ), x, core), tp)
    has_up = z < NZ - 1
    has_dn = z > 0
    counts_copy = pltpu.make_async_copy(counts_hbm, counts, csem)
    counts_copy.start()
    partners = [(dx, dc) for dx in (0, 1, 3, 2) for dc in range(NC) if dx + dc > 0]

    def mate(dx, dc):
        return lax.rem(x + dx, NX), lax.rem(core + dc, NC)

    srcs = ((k, kvs, 0), (v, kvs, 1), (q, qgs, 0), (g, qgs, 1))
    own_parity = lax.rem(core + here, NC)
    own = []
    for a, (src, dst, part) in enumerate(srcs):
        cp = pltpu.make_async_copy(src.at[:, own_parity, :, cols(x)], dst.at[z, core, here, part], loc.at[a])
        cp.start()
        own.append(cp)

    barrier = pltpu.get_barrier_semaphore()
    for dx, dc in partners:
        px, pc = mate(dx, dc)
        pl.semaphore_signal(barrier, inc=1, device_id=(ctx_of(z, px, pc), tp), device_id_type=MESH)
    for dz in range(1, NZ):
        for pc in range(NC):
            pl.semaphore_signal(
                barrier, inc=1, device_id=(ctx_of(lax.rem(z + dz, NZ), x, pc), tp), device_id_type=MESH
            )
    pl.semaphore_wait(barrier, len(partners) + (NZ - 1) * NC)

    sends = []
    for dx, dc in partners:
        px, pc = mate(dx, dc)
        parity = lax.rem(pc + here, NC)
        for a, (src, dst, part) in enumerate(srcs):
            cp = remote(
                src.at[:, parity, :, cols(px)],
                dst.at[z, pc, here, part],
                sa.at[a, dx, dc],
                ra.at[a, dx, dc],
                (ctx_of(z, px, pc), tp),
            )
            cp.start()
            sends.append(cp)

    lane = lax.broadcasted_iota(jnp.int32, (8, SEG), 1)
    for j in range(NS):
        inside = (2 * (lane // BR) + lax.rem(core + j, NC)) * BR + lax.rem(lane, BR)
        qpos_ref[:, j * SEG : (j + 1) * SEG] = (z * NS + j) * CAP + inside
    m_ref[...] = jnp.full(m_ref.shape, -FAR, jnp.float32)
    l_ref[...] = jnp.zeros_like(l_ref)
    acc[...] = jnp.zeros_like(acc)
    dkv[...] = jnp.zeros_like(dkv)
    counts_copy.wait()
    wide_lane = lax.broadcasted_iota(jnp.int32, (8, GROUP), 1)
    wide_sub = lax.broadcasted_iota(jnp.int32, (8, GROUP), 0)

    def begins(p, c):
        at = [jnp.int32(0)]
        for j in range(NS):
            at.append(at[-1] + live_blocks(counts, p, c, j))
        return at

    def describe(n, _):
        p, c = n // NC, lax.rem(n, NC)
        at = begins(p, c)

        def source(b, _):
            shift = jnp.int32(0)
            for j in range(1, NS):
                shift = jnp.where(b >= at[j], j * SB - at[j], shift)
            table[n * (GROUP // BR) + b] = jnp.minimum(b + shift, GROUP // BR - 1)
            return 0

        lax.fori_loop(0, GROUP // BR, source, 0)
        start = jnp.zeros_like(wide_lane)
        shift = jnp.zeros_like(wide_lane) + c * BR
        kept = jnp.zeros_like(wide_lane) + counts[p * NS]
        for j in range(1, NS):
            inside = wide_lane >= at[j] * BR
            start = jnp.where(inside, at[j] * BR, start)
            shift = jnp.where(inside, j * CAP + lax.rem(c + j, NC) * BR, shift)
            kept = jnp.where(inside, j * CAP + counts[p * NS + j], kept)
        t = wide_lane - start
        pos = t + (t // BR) * BR + shift
        bias = jnp.where(pos < kept, 0.0, -FAR)
        info[p, c] = jnp.where(wide_sub == 0, bias, (pos + p * (NS * CAP)).astype(jnp.float32))
        return 0


    def pack(buf, dst, p):
        def group(c, _):
            stage[...] = buf[p, c]

            def step(i, _):
                for b in range(8):
                    n = table[(p * NC + c) * (GROUP // BR) + i * 8 + b]
                    j, r = n // SB, lax.rem(n, SB)
                    for part in range(2):
                        dst[p, c, part, i * 8 + b] = stage[j, part, r]
                return 0

            lax.fori_loop(0, GROUP // BR // 8, step, 0)
            return 0

        lax.fori_loop(0, NC, group, 0)

    def chunk(buf, p, c, xs):
        return buf.at[p, c, pl.ds(2 * xs, 2)]

    def keys_of(p, xs):
        inner = lax.broadcasted_iota(jnp.int32, (SEG, 1), 0)
        ks, vs, keys = [], [], []
        for c in range(NC):
            both = kvs[p, c, pl.ds(2 * xs, 2)]
            ks.append(both[:, 0].reshape(2 * SEG, HD))
            vs.append(both[:, 1].reshape(2 * SEG, HD))
            for jj in range(2):
                inside = (2 * (inner // BR) + (c + jj) % 2) * BR + lax.rem(inner, BR)
                live = inside < counts[p * NS + 2 * xs + jj]
                keys.append(jnp.where(live, (p * NS + 2 * xs + jj) * CAP + inside, BIG))
        kk = jnp.concatenate(ks, axis=0)
        vv = jnp.concatenate(vs, axis=0)
        s = dot(kk, qgs[z, core, :, 0].reshape(GROUP, HD), NT) * SCALE2
        return kk, vv, jnp.where(jnp.concatenate(keys, axis=0) <= qpos_ref[0:1, :], s, -FAR)

    def unit(p, xs):
        _, vv, s = keys_of(p, xs)
        m = m_ref[0:1, :]
        new = jnp.maximum(m, jnp.max(s, axis=0, keepdims=True))
        pr = jnp.exp2(s - new)
        f = jnp.exp2(m - new)
        m_ref[0:1, :] = new
        l_ref[0:1, :] = l_ref[0:1, :] * f + jnp.sum(pr, axis=0, keepdims=True)
        acc[...] = acc[...] * f + dot(vv.T, pr.astype(jnp.bfloat16), NN)

    def unit_back(p, xs):
        kk, vv, s = keys_of(p, xs)
        pr = jnp.exp2(s - m_ref[0:1, :])
        dp = dot(vv, qgs[z, core, :, 1].reshape(GROUP, HD), NT)
        ds = (pr * (dp - l_ref[0:1, :])).astype(jnp.bfloat16)
        acc[...] += dot(kk.T, ds, NN)

    def unit_key(p, xs):
        line = lax.broadcasted_iota(jnp.int32, (1, SEG), 1)
        inner = lax.broadcasted_iota(jnp.int32, (SEG, 1), 0)
        qs, gs, lses, deltas, queries, keys = [], [], [], [], [], []
        for c in range(NC):
            both = qgs[p, c, pl.ds(2 * xs, 2)]
            qs.append(both[:, 0].reshape(2 * SEG, HD))
            gs.append(both[:, 1].reshape(2 * SEG, HD))
            lanes = pl.ds(pl.multiple_of(2 * xs * SEG, 2 * SEG), 2 * SEG)
            lses.append(stv[p, c, 2:3, lanes])
            deltas.append(stv[p, c, 3:4, lanes])
            for jj in range(2):
                inside = (2 * (line // BR) + (c + jj) % 2) * BR + lax.rem(line, BR)
                queries.append((p * NS + 2 * xs + jj) * CAP + inside)
        for j in range(NS):
            keys.append((z * NS + j) * CAP + (2 * (inner // BR) + lax.rem(core + j, NC)) * BR + lax.rem(inner, BR))
        qq, gg = jnp.concatenate(qs, axis=0), jnp.concatenate(gs, axis=0)
        lse, delta = jnp.concatenate(lses, axis=1), jnp.concatenate(deltas, axis=1)
        s = dot(kvs[z, core, :, 0].reshape(GROUP, HD), qq, NT) * SCALE2
        pr = jnp.exp2(s - lse)
        pr = jnp.where(jnp.concatenate(keys, axis=0) <= jnp.concatenate(queries, axis=1), pr, 0.0)
        dkv[1] += dot(pr.astype(jnp.bfloat16), gg, NN)
        dp = dot(kvs[z, core, :, 1].reshape(GROUP, HD), gg, NT)
        dkv[0] += dot((pr * (dp - delta)).astype(jnp.bfloat16), qq, NN)

    flows = ((kvs, -1, has_up, above), (qgs, 1, has_dn, below))

    def place_of(t):
        m = lax.rem(t, NX)
        return t // NX, m, lax.rem(x + NX - (m + m // 2 - 2 * (m // 3)), NX)

    def own_comm(m):
        _, _, xs = place_of(m)
        dx = lax.rem(x + NX - xs, NX)
        for half, (buf, _, has, dev) in enumerate(flows):
            for part in range(2):
                a = 2 * half + part
                for dc in range(NC):
                    ref = buf.at[z, core, xs * NC + lax.rem(core + dc, NC), part]
                    if dc == 0:

                        @pl.when(m == 0)
                        def _():
                            own[a].wait()

                        @pl.when(m > 0)
                        def _():
                            remote(ref, ref, sa.at[a, dx, dc], ra.at[a, dx, dc], sib).wait_recv()

                    else:
                        remote(ref, ref, sa.at[a, dx, dc], ra.at[a, dx, dc], sib).wait_recv()
            ref = chunk(buf, z, core, xs)

            @pl.when(has)
            def _():
                remote(ref, ref, sown.at[half, m], rz.at[z, m], dev).start()

            remote(ref, ref, sso.at[half, m], rso.at[half, m], sib).start()

    def comm(t):
        d, m, xs = place_of(t)
        for buf, sign, has, dev in flows:
            p = z + sign * (d + 1)

            @pl.when((p >= 0) & (p < NZ))
            def _():
                ref = chunk(buf, p, core, xs)
                remote(ref, ref, sfw.at[p, m], rz.at[p, m], sib).wait_recv()

                @pl.when(has)
                def _():
                    remote(ref, ref, sfw.at[p, m], rz.at[p, m], dev).start()

                remote(ref, ref, ssf.at[p, m], rs.at[p, m], sib).start()

    def work(u, _):
        d, m, xs = place_of(u)

        @pl.when(d == 0)
        def _():
            for half, (buf, _, has, dev) in enumerate(flows):
                ref = chunk(buf, z, 1 - core, xs)
                remote(ref, ref, sso.at[half, m], rso.at[half, m], sib).wait_recv()

        for buf, sign, has, dev in flows:
            p = z + sign * d

            @pl.when((d > 0) & (p >= 0) & (p < NZ))
            def _():
                ref = chunk(buf, p, 1 - core, xs)
                remote(ref, ref, ssf.at[p, m], rs.at[p, m], sib).wait_recv()

        @pl.when(z - d >= 0)
        def _():
            unit(z - d, xs)

        whole = (m == NX - 1) & (d < NZ - 1)

        @pl.when(whole & ((d == 0) | (z == NZ - 1)))
        def _():
            pack(kvs, kvp, z - d)

        @pl.when(whole & (z + d < NZ) & ((z > 1) | (z + d == NZ - 1)))
        def _():
            pack(qgs, qgp, z + d)

        return 0

    def own_step(m, _):
        own_comm(m)
        describe(2 * m, 0)
        describe(2 * m + 1, 0)
        return 0

    stats = stv.at[z, core]

    def send_stats(act):
        act(remote(stats, stats, sst.at[0], rst.at[z, core], sib))
        for dz in range(1, NZ):

            @pl.when(z - dz >= 0)
            def _():
                for pc in range(NC):
                    dev = (ctx_of(z - dz, x, pc), tp)
                    act(remote(stats, stats, sst.at[dz * NC + pc], rst.at[z, core], dev))

    def send_rows(act):
        for dx, dc in partners:
            px, pc = mate(dx, dc)
            there = px * NC + pc
            parity = lax.rem(core + there, NC)
            act(
                remote(
                    oc.at[there], att.at[x, :, parity], sat.at[dx, dc], rat.at[dx, dc], (ctx_of(z, px, pc), tp)
                )
            )

    stay = pltpu.make_async_copy(oc.at[here], att.at[x, :, own_parity], lat)

    def finish():
        sub = lax.broadcasted_iota(jnp.int32, (8, SEG), 0)
        at = begins(z, core)
        packed = jnp.where(wide_sub == 0, FAR, 0.0)
        for j in range(NS):
            rows = slice(j * SEG, (j + 1) * SEG)
            live = qpos_ref[0:1, rows] - (z * NS + j) * CAP < counts[z * NS + j]
            l = l_ref[0:1, rows]
            o = jnp.where(live, acc[:, rows] / l, 0.0).T.astype(jnp.bfloat16)
            oc[j] = o.reshape(SB, BR, HD)
            cot = qgs[z, core, j, 1].reshape(SEG, HD).astype(jnp.float32)
            delta = jnp.sum(o.astype(jnp.float32) * cot, axis=1, keepdims=True)
            lse = jnp.where(live, m_ref[0:1, rows] + jnp.log2(l), FAR)
            both = jnp.where(sub == 0, lse, jnp.broadcast_to(delta, (SEG, HD)).T[:8, :])
            m_ref[0:1, rows] = lse
            l_ref[0:1, rows] = both[1:2, :]
            both = jnp.concatenate([both, jnp.zeros((8, GROUP - SEG), jnp.float32)], axis=1)
            inside = (wide_lane >= at[j] * BR) & (wide_lane < at[j + 1] * BR)
            packed = jnp.where(inside, pltpu.roll(both, at[j] * BR, 1), packed)
        dense = jnp.where(wide_sub == 2, m_ref[0:1, :], l_ref[0:1, :])
        stv[z, core] = jnp.where(wide_sub < 2, packed, dense)
        for j in range(NS):
            rows = slice(j * SEG, (j + 1) * SEG)
            block = jnp.concatenate([packed[:, rows], jnp.zeros((SEG - 8, SEG), jnp.float32)], axis=0)
            col[rows, :] = block.T

        acc[...] = jnp.zeros_like(acc)
        send_stats(lambda cp: cp.start())
        send_rows(lambda cp: cp.start())
        stay.start()

    top = z == NZ - 1
    done = jnp.where(z == 0, 1, 4 * z - 1)
    pace = jnp.where(z == NZ - 2, 3, jnp.where(z == 1, 2, 1))

    def back(u, _):
        d, m, xs = place_of(u)
        unit_back(z - d, xs)
        return 0

    def key_work(w, _):
        d, m, xs = place_of(w)
        p = z + d
        for c in range(NC):

            @pl.when((m == 0) & ((d > 0) | (c != core)))
            def _():
                ref = stv.at[p, c]
                remote(ref, ref, sst.at[0], rst.at[p, c], sib).wait_recv()

        unit_key(p, xs)
        return 0

    def step(t, _):
        @pl.when(t < (NZ - 1) * NX)
        def _():
            comm(t)

        lax.fori_loop(jnp.where(t < 4, 2 * t, t + 4), jnp.where(t < 4, 2 * t + 2, t + 5), work, 0)

        @pl.when(t == done)
        def _():
            finish()

        @pl.when((t > done) & (z < NZ - 1))
        def _():
            first = (t - done - 1) * pace
            last = jnp.maximum(first, jnp.minimum(first + pace, NX * (z + 1)))
            lax.fori_loop(first, last, back, 0)

        start = jnp.where(z == 0, 6, 8)

        @pl.when((z <= 1) & (t >= start) & (t < start + 2 * (NZ - 1 - z)))
        def _():
            lax.fori_loop(2 * (t - start), 2 * (t - start) + 2, key_work, 0)

        return 0

    lax.fori_loop(0, NX, own_step, 0)
    lax.fori_loop(0, (NZ - 1) * NX, step, 0)

    @pl.when(z < NZ - 1)
    def _():
        for j in range(NS):
            rows = slice(j * SEG, (j + 1) * SEG)
            dqs[j] = (acc[:, rows] * SCALE).T.astype(jnp.bfloat16).reshape(SB, BR, HD)
        pltpu.make_async_copy(dqs, dq_out, sdq).start()

    @pl.when(z <= 1)
    def _():
        pltpu.make_async_copy(dkv, dkv_out, sdkv).start()

    @pl.when(z == NZ - 1)
    def _():
        pack(kvs, kvp, 0)

    @pl.when(z == 0)
    def _():
        pack(qgs, qgp, NZ - 1)

    outs = [
        pltpu.make_async_copy(col, col_out, ost.at[NZ, 0]),
        pltpu.make_async_copy(info, info_out, ost.at[NZ, 1]),
    ]
    for buf, dst, sem in ((kvp, kv_out, okv), (qgp, qg_out, oqg)):
        outs.append(pltpu.make_async_copy(buf.at[z], dst.at[z], sem.at[z]))
    for cp in outs:
        cp.start()
    def copies(act, take):
        for dz in range(1, NZ):

            @pl.when((z - dz >= 0) & (z == NZ - 1))
            def _():
                act(pltpu.make_async_copy(kvp.at[z - dz], kv_out.at[z - dz], okv.at[z - dz]))

            @pl.when((z + dz < NZ) & ((z > 1) | (z + dz == NZ - 1)))
            def _():
                act(pltpu.make_async_copy(qgp.at[z + dz], qg_out.at[z + dz], oqg.at[z + dz]))

        @pl.when(z > 1)
        def _():
            act(pltpu.make_async_copy(stats, st_out.at[z, core], ost.at[z, core]))
            take(z, 1 - core)

        for dz in range(1, NZ):

            @pl.when((z + dz < NZ) & ((z > 1) | (z + dz == NZ - 1)))
            def _():
                for c in range(NC):
                    take(z + dz, c)

    def take(p, c):
        ref = stv.at[p, c]
        remote(ref, ref, sst.at[0], rst.at[p, c], sib).wait_recv()
        pltpu.make_async_copy(ref, st_out.at[p, c], ost.at[p, c]).start()

    copies(lambda cp: cp.start(), take)

    for cp in outs:
        cp.wait()
    stay.wait()
    for dx, dc in partners:
        ox, oc_ = lax.rem(x + NX - dx, NX), lax.rem(core + NC - dc, NC)
        parity = lax.rem(oc_ + here, NC)
        ref = att.at[ox, :, parity]
        remote(oc.at[here], ref, sat.at[dx, dc], rat.at[dx, dc], sib).wait_recv()
    for cp in sends:
        cp.wait_send()
    send_rows(lambda cp: cp.wait_send())
    send_stats(lambda cp: cp.wait_send())

    @pl.when(z < NZ - 1)
    def _():
        pltpu.make_async_copy(dqs, dq_out, sdq).wait()

    @pl.when(z <= 1)
    def _():
        pltpu.make_async_copy(dkv, dkv_out, sdkv).wait()

    copies(
        lambda cp: cp.wait(),
        lambda p, c: pltpu.make_async_copy(stv.at[p, c], st_out.at[p, c], ost.at[p, c]).wait(),
    )

    for m in range(NX):
        _, _, xs = place_of(jnp.int32(m))
        for half, (buf, _, has, dev) in enumerate(flows):
            ref = chunk(buf, z, core, xs)

            @pl.when(has)
            def _():
                remote(ref, ref, sown.at[half, m], rz.at[z, m], dev).wait_send()

            remote(ref, ref, sso.at[half, m], rso.at[half, m], sib).wait_send()

    def sent(t, _):
        d, m, xs = place_of(t)
        for buf, sign, has, dev in flows:
            p = z + sign * (d + 1)

            @pl.when((p >= 0) & (p < NZ))
            def _():
                ref = chunk(buf, p, core, xs)

                @pl.when(has)
                def _():
                    remote(ref, ref, sfw.at[p, m], rz.at[p, m], dev).wait_send()

                remote(ref, ref, ssf.at[p, m], rs.at[p, m], sib).wait_send()

        return 0

    lax.fori_loop(0, (NZ - 1) * NX, sent, 0)


WHOLE = (NZ, NC, NS, 2, SB, BR, HD)
PACKED = (NZ, NC, 2, GROUP // BR, BR, HD)
ROWS = (NZ, NC, 8, GROUP)
LANDED = jax.ShapeDtypeStruct((NX, SB, 2, BR, HD), jnp.bfloat16)
PARTS = jax.ShapeDtypeStruct((NS, SB, BR, HD), jnp.bfloat16)
GRADS = jax.ShapeDtypeStruct((NS, 3, SB, BR, HD), jnp.bfloat16)
LANDED3 = jax.ShapeDtypeStruct((NX, 3, SB, 2, BR, HD), jnp.bfloat16)


def attend(q, k, v, g, counts):
    dma = pltpu.SemaphoreType.DMA
    packed = jax.ShapeDtypeStruct(PACKED, jnp.bfloat16)
    rows = jax.ShapeDtypeStruct(ROWS, jnp.float32)
    return pl.pallas_call(
        attend_kernel,
        out_shape=(
            packed,
            packed,
            LANDED,
            rows,
            rows,
            jax.ShapeDtypeStruct((GROUP, HD), jnp.float32),
            PARTS,
            jax.ShapeDtypeStruct((2, GROUP, HD), jnp.float32),
        ),
        in_specs=[HBM] * 5,
        out_specs=(HBM,) * 8,
        scratch_shapes=[
            pltpu.VMEM(WHOLE, jnp.bfloat16),
            pltpu.VMEM(WHOLE, jnp.bfloat16),
            pltpu.VMEM((NS, 2, SB, BR, HD), jnp.bfloat16),
            pltpu.VMEM((NS, SB, BR, HD), jnp.bfloat16),
            pltpu.VMEM((2, GROUP, HD), jnp.float32),
            pltpu.VMEM(PACKED, jnp.bfloat16),
            pltpu.VMEM(PACKED, jnp.bfloat16),
            pltpu.VMEM(ROWS, jnp.float32),
            pltpu.VMEM(ROWS, jnp.float32),
            pltpu.VMEM((GROUP, HD), jnp.float32),
            pltpu.VMEM((NS, SB, BR, HD), jnp.bfloat16),
            pltpu.VMEM((8, GROUP), jnp.float32),
            pltpu.VMEM((8, GROUP), jnp.float32),
            pltpu.VMEM((HD, GROUP), jnp.float32),
            pltpu.VMEM((8, GROUP), jnp.int32),
            pltpu.SMEM((NZ * NS,), jnp.int32),
            pltpu.SMEM((NZ * NC * (GROUP // BR),), jnp.int32),
            dma,
            dma((4,)),
            dma((4, NX, NC)),
            dma((4, NX, NC)),
            dma((2, NX)),
            dma((2, NX)),
            dma((2, NX)),
            dma((NZ, NX)),
            dma((NZ, NX)),
            dma((NZ, NX)),
            dma((NZ, NX)),
            dma((NZ * NC,)),
            dma((NZ, NC)),
            dma((NX, NC)),
            dma((NX, NC)),
            dma,
            dma((NZ,)),
            dma((NZ,)),
            dma((NZ + 1, NC)),
            dma,
            dma,
        ],
        compiler_params=pltpu.CompilerParams(
            collective_id=0, has_side_effects=True, vmem_limit_bytes=VMEM_BYTES
        ),
        name="attend",
    )(q, k, v, g, counts)


def return_kernel(grads, out, loc, ssem, rsem):
    z, x, core, tp = place()
    here = x * NC + core
    partners = [(dx, dc) for dx in (2, 1, 3, 0) for dc in range(NC) if dx + dc > 0]
    own = pltpu.make_async_copy(grads.at[here], out.at[x, :, :, lax.rem(core + here, NC)], loc)
    own.start()
    barrier = pltpu.get_barrier_semaphore()
    for dx, dc in partners:
        dev = (ctx_of(z, lax.rem(x + dx, NX), lax.rem(core + dc, NC)), tp)
        pl.semaphore_signal(barrier, inc=1, device_id=dev, device_id_type=MESH)
    pl.semaphore_wait(barrier, len(partners))
    sends = []
    for dx, dc in partners:
        px, pc = lax.rem(x + dx, NX), lax.rem(core + dc, NC)
        there = px * NC + pc
        cp = remote(
            grads.at[there],
            out.at[x, :, :, lax.rem(core + there, NC)],
            ssem.at[dx, dc],
            rsem.at[dx, dc],
            (ctx_of(z, px, pc), tp),
        )
        cp.start()
        sends.append(cp)
    own.wait()
    for dx, dc in partners:
        ox, oc = lax.rem(x + NX - dx, NX), lax.rem(core + NC - dc, NC)
        ref = out.at[ox, :, :, lax.rem(oc + here, NC)]
        remote(grads.at[here], ref, ssem.at[dx, dc], rsem.at[dx, dc], (ctx_of(z, ox, oc), tp)).wait_recv()
    for cp in sends:
        cp.wait_send()


def return_heads(grads):
    dma = pltpu.SemaphoreType.DMA
    return pl.pallas_call(
        return_kernel,
        out_shape=LANDED3,
        in_specs=[HBM],
        out_specs=HBM,
        scratch_shapes=[dma, dma((NX, NC)), dma((NX, NC))],
        compiler_params=pltpu.CompilerParams(collective_id=1, has_side_effects=True),
        name="return_heads",
    )(grads)


def assemble_kernel(att, grads, *refs):
    outs = refs[:4]
    buf0, buf, res, lsem, ssem = refs[4:]
    loads = [pltpu.make_async_copy(att, buf0, lsem.at[0])]
    loads += [pltpu.make_async_copy(grads.at[:, a], buf.at[:, a], lsem.at[a + 1]) for a in range(3)]
    for cp in loads:
        cp.start()
    stores = [pltpu.make_async_copy(res.at[a], outs[a], ssem.at[a]) for a in range(4)]
    for a in range(4):
        loads[a].wait()
        for i in range(NX):
            part = buf0[i] if a == 0 else buf[i, a - 1]
            res[a, :, i * HD : (i + 1) * HD] = part.reshape(CAP, HD)
        stores[a].start()
    for cp in stores:
        cp.wait()


def assemble(att, grads):
    dma = pltpu.SemaphoreType.DMA
    shape = jax.ShapeDtypeStruct((CAP, NX * HD), jnp.bfloat16)
    return pl.pallas_call(
        assemble_kernel,
        out_shape=(shape,) * 4,
        in_specs=[HBM] * 2,
        out_specs=(HBM,) * 4,
        scratch_shapes=[
            pltpu.VMEM(LANDED.shape, jnp.bfloat16),
            pltpu.VMEM(LANDED3.shape, jnp.bfloat16),
            pltpu.VMEM((4, CAP, NX * HD), jnp.bfloat16),
            dma((4,)),
            dma((4,)),
        ],
        compiler_params=pltpu.CompilerParams(vmem_limit_bytes=VMEM_BYTES),
        name="assemble",
    )(att, grads)


def fill_offsets(counts, off, z, sign, planes):
    def step(n, at):
        off[n] = at
        p, c = z + sign * (n // NC), lax.rem(n, NC)
        for j in range(NS):
            at = at + live_blocks(counts, p, c, j)
        return at

    off[planes * NC] = lax.fori_loop(0, planes * NC, step, jnp.int32(0))


def load(off, src, dst, sem, z, sign, planes, wait):
    def step(n, _):
        at = off[n]
        blocks = off[n + 1] - at
        cp = pltpu.make_async_copy(
            src.at[z + sign * (n // NC), lax.rem(n, NC), :, pl.ds(0, blocks)],
            dst.at[:, pl.ds(at, blocks)],
            sem.at[n],
        )
        if wait:
            cp.wait()
        else:
            cp.start()
        return 0

    lax.fori_loop(0, planes * NC, step, 0)


def line_up(off, src, dst, z, sign, planes, tail):
    width = GROUP + 128
    lane = lax.broadcasted_iota(jnp.int32, (8, width), 1)
    sub = lax.broadcasted_iota(jnp.int32, (8, 128), 0)

    def step(n, _):
        to = off[n] * BR
        at = pl.multiple_of((to // 128) * 128, 128)
        new = src[z + sign * (n // NC), lax.rem(n, NC)]
        new = pltpu.roll(jnp.concatenate([new, jnp.zeros((8, 128), jnp.float32)], axis=1), to - at, 1)
        old = dst[:, pl.ds(at, width)]
        dst[:, pl.ds(at, width)] = jnp.where(lane >= to - at, new, old)
        return 0

    lax.fori_loop(0, planes * NC, step, 0)
    total = off[planes * NC] * BR
    blank = jnp.where(sub == 0, tail, 0.0)
    for t in range(T // 128 + 1):
        at = pl.multiple_of((total // 128 + t) * 128, 128)
        old = dst[:, pl.ds(at, 128)]
        dst[:, pl.ds(at, 128)] = jnp.where(at + lane[:, :128] >= total, blank, old)


def backward_kernel(
    counts_hbm, qg, kv, st, info, stcol, dq_in, dkv_in, grads,
    counts, koff, qoff, kvc, qgc, stv, infov, qrow, krow, col, dqa, dka, dva, res, dkv, begin,
    csem, ksem, qsem, ssem, osem,
):
    z, x, core, _ = place()
    cp = pltpu.make_async_copy(counts_hbm, counts, csem)
    cp.start()
    smalls = [
        pltpu.make_async_copy(src, dst, ssem.at[i])
        for i, (src, dst) in enumerate(((st, stv), (info, infov), (stcol, col)))
    ]
    for small in smalls:
        small.start()
    cp.wait()
    top = z == NZ - 1
    early = pltpu.make_async_copy(dq_in, res.at[:, 0], osem.at[0])

    @pl.when(z < NZ - 1)
    def _():
        early.start()

    dkv_copy = pltpu.make_async_copy(dkv_in, dkv, osem.at[2])

    @pl.when(z <= 1)
    def _():
        dkv_copy.start()

    @pl.when(z > 1)
    def _():
        def clear(j, _):
            for part in range(2):
                dkv[part, pl.ds(pl.multiple_of(j * SEG, SEG), SEG), :] = jnp.zeros((SEG, HD), jnp.float32)
            return 0

        lax.fori_loop(0, NS, clear, 0)

    zq = jnp.where(z <= 1, NZ - 1, z)
    kplanes, qplanes = jnp.where(top, NZ, 1), NZ - zq
    fill_offsets(counts, koff, z, -1, kplanes)
    load(koff, kv, kvc, ksem, z, -1, kplanes, False)
    fill_offsets(counts, qoff, zq, 1, qplanes)
    load(qoff, qg, qgc, qsem, zq, 1, qplanes, False)
    key_end = koff[kplanes * NC]
    query_end = qoff[qplanes * NC]
    plane_end = jnp.where(z <= 1, 0, koff[NC])
    zero = jnp.zeros((GROUP // BR, BR, HD), jnp.bfloat16)
    for part in range(2):
        kvc[part, pl.ds(key_end, GROUP // BR)] = zero
        qgc[part, pl.ds(query_end, GROUP // BR)] = zero
    for small in smalls:
        small.wait()
    line_up(koff, infov, krow, z, -1, kplanes, -FAR)
    line_up(qoff, stv, qrow, zq, 1, qplanes, FAR)
    base = koff[core]
    total = koff[core + 1] - base
    starts = [jnp.int32(0)]
    for j in range(NS):
        starts.append(starts[-1] + live_blocks(counts, z, core, j))
        begin[j] = starts[j]
    load(koff, kv, kvc, ksem, z, -1, kplanes, True)
    load(qoff, qg, qgc, qsem, zq, 1, qplanes, True)

    def tile(buf, part, t):
        return buf[part, pl.ds(t * (T // BR), T // BR)].reshape(T, HD)

    def run(M):
        rows = pl.ds(base, M // BR)
        r = lax.broadcasted_iota(jnp.int32, (M, 1), 0)
        start = jnp.zeros_like(r)
        shift = jnp.zeros_like(r) + lax.rem(core, NC) * BR
        for j in range(1, NS):
            inside = r >= starts[j] * BR
            start = jnp.where(inside, starts[j] * BR, start)
            shift = jnp.where(inside, j * CAP + lax.rem(core + j, NC) * BR, shift)
        t = r - start
        pos = (t + (t // BR) * BR + shift + z * (NS * CAP)).astype(jnp.float32)

        dka[0:M, :] = jnp.zeros((M, HD), jnp.float32)
        dva[0:M, :] = jnp.zeros((M, HD), jnp.float32)
        dqa[0:M, :] = jnp.zeros((M, HD), jnp.float32)

        def key_step(qt, _):
            lanes = pl.ds(pl.multiple_of(qt * T, T), T)
            qb, gb = tile(qgc, 0, qt), tile(qgc, 1, qt)
            p = jnp.exp2(dot(kvc[0, rows].reshape(M, HD), qb, NT) * SCALE2 - qrow[0:1, lanes])
            n = qt * T + lax.broadcasted_iota(jnp.int32, (1, T), 1)
            there = jnp.where(n < plane_end * BR, krow[1:2, lanes], FAR)
            p = jnp.where(pos <= there, p, 0.0)
            dva[0:M, :] += dot(p.astype(jnp.bfloat16), gb, NN)
            dp = dot(kvc[1, rows].reshape(M, HD), gb, NT)
            ds = (p * (dp - qrow[1:2, lanes])).astype(jnp.bfloat16)
            dka[0:M, :] += dot(ds, qb, NN)
            return 0

        def query_step(kt, _):
            lanes = pl.ds(pl.multiple_of(kt * T, T), T)
            kb, vb = tile(kvc, 0, kt), tile(kvc, 1, kt)
            s = dot(qgc[0, rows].reshape(M, HD), kb, NT) * SCALE2 + krow[0:1, lanes]
            s = jnp.where(krow[1:2, lanes] <= pos, s, -FAR)
            p = jnp.exp2(s - col[0:M, 0:1])
            dp = dot(qgc[1, rows].reshape(M, HD), vb, NT)
            dqa[0:M, :] += dot((p * (dp - col[0:M, 1:2])).astype(jnp.bfloat16), kb, NN)
            return 0

        per = T // BR
        lax.fori_loop(0, (query_end + per - 1) // per, key_step, 0)
        lax.fori_loop(0, jnp.where(top, (key_end + per - 1) // per, 0), query_step, 0)

    lower = 0
    for size in SIZES:

        @pl.when((total * BR > lower) & (total * BR <= size))
        def _():
            run(size)

        lower = size

    r = lax.broadcasted_iota(jnp.int32, (SEG, HD), 0)

    def spread(a, src, scale, more):
        def step(j, _):
            row = r + (r // BR + lax.rem(core + j, NC)) * BR
            part = src[pl.ds(pl.multiple_of(begin[j] * BR, BR), SEG), :]
            if more is not None:
                part = part + dkv[more, pl.ds(pl.multiple_of(j * SEG, SEG), SEG), :]
            part = jnp.where(row < counts[z * NS + j], part * scale, 0.0)
            res[j, a] = part.astype(jnp.bfloat16).reshape(SB, BR, HD)
            return 0

        lax.fori_loop(0, NS, step, 0)

    @pl.when(z <= 1)
    def _():
        dkv_copy.wait()

    spread(1, dka, SCALE, 0)
    spread(2, dva, 1.0, 1)

    @pl.when(top)
    def _():
        spread(0, dqa, SCALE, None)

    @pl.when(z < NZ - 1)
    def _():
        early.wait()

    store = pltpu.make_async_copy(res, grads, osem.at[1])
    store.start()
    store.wait()


def backward(counts, qg, kv, st, info, stcol, dq, dkv):
    dma = pltpu.SemaphoreType.DMA
    blocks = (KEYS + GROUP + T) // BR
    return pl.pallas_call(
        backward_kernel,
        out_shape=GRADS,
        in_specs=[HBM] * 8,
        out_specs=HBM,
        scratch_shapes=[
            pltpu.SMEM((NZ * NS,), jnp.int32),
            pltpu.SMEM((NZ * NC + 1,), jnp.int32),
            pltpu.SMEM((NZ * NC + 1,), jnp.int32),
            pltpu.VMEM((2, blocks, BR, HD), jnp.bfloat16),
            pltpu.VMEM((2, blocks, BR, HD), jnp.bfloat16),
            pltpu.VMEM(ROWS, jnp.float32),
            pltpu.VMEM(ROWS, jnp.float32),
            pltpu.VMEM((8, KEYS + GROUP + T), jnp.float32),
            pltpu.VMEM((8, KEYS + GROUP + T), jnp.float32),
            pltpu.VMEM((GROUP, HD), jnp.float32),
            pltpu.VMEM((GROUP + SEG, HD), jnp.float32),
            pltpu.VMEM((GROUP + SEG, HD), jnp.float32),
            pltpu.VMEM((GROUP + SEG, HD), jnp.float32),
            pltpu.VMEM(GRADS.shape, jnp.bfloat16),
            pltpu.VMEM((2, GROUP, HD), jnp.float32),
            pltpu.SMEM((NS,), jnp.int32),
            dma,
            dma((NZ * NC,)),
            dma((NZ * NC,)),
            dma((3,)),
            dma((3,)),
        ],
        compiler_params=pltpu.CompilerParams(vmem_limit_bytes=VMEM_BYTES),
        name="backward",
    )(counts, qg, kv, st, info, stcol, dq, dkv)


def on_device(query_heads, key_heads, value_heads, grad_heads, counts):
    def blocks(array):
        return array.reshape(SB, 2, BR, NX * HD)

    kv, qg, att, st, info, stcol, dq, dkv = attend(
        blocks(query_heads), blocks(key_heads), blocks(value_heads), blocks(grad_heads), counts
    )
    grads = backward(counts, qg, kv, st, info, stcol, dq, dkv)
    return tuple(assemble(att, return_heads(grads)))


def solution(mesh):
    return jax.shard_map(
        on_device,
        mesh=mesh,
        in_specs=(P("ctx", "tp"), P("ctx", "tp"), P("ctx", "tp"), P("ctx", "tp"), P()),
        out_specs=(P("ctx", "tp"), P("ctx", "tp"), P("ctx", "tp"), P("ctx", "tp")),
        check_vma=False,
    )
```
